128 devices in a mesh: row: 8 (over z, x_hi), col: 16 (over x_lo, y, core).
Axes of the slice: x: 4 (x_hi: 2, x_lo: 2; x = x_hi * 2 + x_lo), y: 4, z: 4, core: 2. Of those that a mesh axis runs over, the one named last changes fastest.
Arguments:
- cycle_cells: int32 [2, 16384], P(None, ('row', 'col')), may hold values from 0 to 1023, as said below
- cycle_offsets: float32 [2, 16384], P(None, ('row', 'col')), may hold values from 0 to 1
- cycle_strength: float32 [16384], P(('row', 'col')), may hold values from -48 to 48
- block_tile: int32 [8192], P(('row', 'col')), may hold values from 0 to 127, as said below
Outputs:
- displacement: float32 [2, 16384], P(None, ('row', 'col'))
- diffused: float32 [4096, 8192], P('col', 'row')
- renewed: float32 [16384], P(('row', 'col'))
The draws below stay inside these ranges and needn't reach their ends.
Inputs may be any that keep to these rules, and one draw needn't show every extreme that they name: Block b's cycles lie in the tile with slab block_tile[b] // 16 and radial part block_tile[b] mod 16. The blocks of one device name one tile at most 2 times and one slab at most 2 * 16 times; in every draw some slab is named 2 * 16 times by every device, each of its tiles twice. `cycle_cells`: row 0 is a radial cell within the cycle's tile, below 256; row 1 an axial cell, below 1024.
All inputs are finite; a program needn't handle non-finite values.
Results may differ from the reference program's by a relative error of at most 0.0004.
Values sent between devices are 32-bit elements; how exact they have to be, the bound alone decides.
A program may use at most 64 MiB of HBM per device.

```python
import math
import jax
import jax.numpy as jnp
from jax import lax

CR = 256
CZ = 1024
CYCLE_DEV = 128
BLK = 2
AGM_STEPS = 6
NR = 4096
NZ = 8192
CYCLES = 16384
N_ROW = 8
N_COL = 16


def shuffled_rows(seed_key, row_total, length):
    many_keys = jax.random.split(seed_key, row_total)
    return jax.vmap(lambda one_key: jax.random.permutation(one_key, length))(many_keys)


def draw_block_tile(key, part):
    devices = N_ROW * N_COL
    blocks = CYCLE_DEV // BLK
    other_slabs = max(N_ROW - 1, 1)
    base_key = jax.random.fold_in(key, 5)
    hot_key, first_key, rest_key, rotation_key, order_key = jax.random.split(base_key, 5)
    hot_slab = jax.random.randint(hot_key, (), 0, N_ROW)
    first_parts = shuffled_rows(first_key, devices, N_COL)
    rest_parts = shuffled_rows(rest_key, devices * N_ROW, N_COL).reshape(devices, N_ROW, N_COL)
    rotation = jax.random.randint(rotation_key, (devices, 1), 0, other_slabs)
    block_number = jnp.arange(blocks, dtype=jnp.int32)[None, :]
    is_hot = block_number < 2 * N_COL
    later_index = jnp.maximum(block_number - 2 * N_COL, 0)
    rest_slab = (hot_slab + 1 + (later_index + rotation) % other_slabs) % N_ROW
    rest_index = jnp.broadcast_to(later_index // other_slabs % N_COL, (devices, blocks))
    device_rows = jnp.broadcast_to(jnp.arange(devices, dtype=jnp.int32)[:, None], (devices, blocks))
    rest_part = rest_parts[device_rows, rest_slab, rest_index]
    hot_part = first_parts[:, jnp.minimum(block_number[0], 2 * N_COL - 1) // 2]
    slab_index = jnp.where(is_hot, hot_slab, rest_slab)
    chosen_part = jnp.where(is_hot, hot_part, rest_part)
    tile_index = slab_index * N_COL + chosen_part
    block_order = shuffled_rows(order_key, devices, blocks)
    tile_index = jnp.take_along_axis(tile_index, block_order, axis=1)
    return tile_index.reshape(-1).astype(jnp.int32)


def draw_cycle_cells(key, part):
    cycle_total = CYCLE_DEV * N_ROW * N_COL
    base_key = jax.random.fold_in(key, 9)
    radial_key, axial_key, edge_radial, edge_axial = jax.random.split(base_key, 4)
    cycle_number = jnp.arange(cycle_total, dtype=jnp.int32)
    radial = jax.random.randint(radial_key, (cycle_total,), 0, CR)
    axial = jax.random.randint(axial_key, (cycle_total,), 0, CZ)
    radial_edge = jax.random.randint(edge_radial, (cycle_total,), 0, 2) * (CR - 1)
    axial_edge = jax.random.randint(edge_axial, (cycle_total,), 0, 2) * (CZ - 1)
    radial = jnp.where(cycle_number % 8 == 0, radial_edge, radial)
    axial = jnp.where(cycle_number % 8 == 4, axial_edge, axial)
    return jnp.stack([radial, axial]).astype(jnp.int32)


def block_levels(rng, dims, shards, smallest, high):
    gain = 1.0
    for position, parts in shards:
        draws = jax.random.uniform(jax.random.fold_in(jax.random.fold_in(rng, 6), position), (parts,), jnp.float32, smallest / len(shards), high / len(shards))
        gain = gain * jnp.repeat(jnp.exp(draws), dims[position] // parts).reshape((-1,) + (1,) * (len(dims) - 1 - position))
    return gain


def centred(rng, extent, deviation, bound, cuts=(), kind=jnp.bfloat16):
    entries = deviation * jax.random.normal(rng, extent, jnp.float32)
    if cuts:
        entries = entries * block_levels(rng, extent, cuts, -0.22, 0.18)
    return jnp.clip(entries, -bound, bound).astype(kind)


def setup_inputs(seed: int = 0) -> dict:
    keys = jax.random.split(jax.random.key(seed), 5)
    return {
        "cycle_cells": draw_cycle_cells(jax.random.fold_in(keys[4], 71), 0),
        "cycle_offsets": jnp.clip(1.0 * jax.random.uniform(keys[1], (2, CYCLES), jnp.float32) ** block_levels(keys[1], (2, CYCLES), ((1, 128),), -0.2, 0.2), 0.0, 1.0),
        "cycle_strength": centred(keys[2], (CYCLES,), 8.0, 48.0, ((0, 128),), jnp.float32),
        "block_tile": draw_block_tile(jax.random.fold_in(keys[4], 71), 0),
    }


CORE_SQUARE = 4.0
STEP_LENGTH = 4.0
VISCOSITY = 0.2

def tent_weight(distance):
    return jnp.maximum(1.0 - jnp.abs(distance), 0.0)

def pair_sums(targets, sources):
    target_r = targets[0][:, None]
    target_z = targets[1][:, None]
    source_r = sources[0][None, :]
    source_z = sources[1][None, :]
    source_gamma = sources[2][None, :]
    axial_gap = target_z - source_z
    smooth_sq = axial_gap * axial_gap + CORE_SQUARE
    radius_sum = target_r + source_r
    radius_gap = target_r - source_r
    far_sq = radius_sum * radius_sum + smooth_sq
    near_sq = radius_gap * radius_gap + smooth_sq
    modulus_sq = 4.0 * target_r * source_r / far_sq
    upper_mean = jnp.ones_like(far_sq)
    lower_mean = jnp.sqrt(near_sq / far_sq)
    series = 0.5 * modulus_sq
    factor = 1.0
    for agm_step in range(AGM_STEPS):
        half_gap = 0.5 * (upper_mean - lower_mean)
        upper_mean, lower_mean = (0.5 * (upper_mean + lower_mean), jnp.sqrt(upper_mean * lower_mean))
        series = series + factor * half_gap * half_gap
        factor = factor * 2.0
    kind_first = 0.5 * math.pi / upper_mean
    kind_second = kind_first * (1.0 - series)
    prefactor = source_gamma / (2.0 * math.pi * jnp.sqrt(far_sq))
    square_sum = source_r * source_r + target_r * target_r + smooth_sq
    square_gap = source_r * source_r - target_r * target_r - smooth_sq
    axial_part = prefactor * (kind_first + square_gap / near_sq * kind_second)
    radial_part = prefactor * axial_gap / target_r * (square_sum / near_sq * kind_second - kind_first)
    return jnp.stack([lax.optimization_barrier(jnp.sum(radial_part, axis=1)), lax.optimization_barrier(jnp.sum(axial_part, axis=1))])

def cycle_velocity(targets, sources):
    target_count = targets.shape[1]
    block_width = 512 if target_count % 512 == 0 else target_count
    grouped = targets.reshape(2, target_count // block_width, block_width).transpose(1, 0, 2)
    result = lax.map(lambda target_group: pair_sums(target_group, sources), grouped)
    return result.transpose(1, 0, 2).reshape(2, target_count)

def diffuse(padded, first_row):
    center = padded[1:-1, 1:-1]
    outward = padded[2:, 1:-1]
    inward = padded[:-2, 1:-1]
    forward_z = padded[1:-1, 2:]
    backward_z = padded[1:-1, :-2]
    radius = jnp.maximum(first_row + jnp.arange(center.shape[0], dtype=jnp.int32), 1).astype(jnp.float32)[:, None]
    laplace = outward + inward + forward_z + backward_z - 4.0 * center + (outward - inward) / (2.0 * radius) - center / (radius * radius)
    return center + VISCOSITY * laplace

def reference(cycle_cells, cycle_offsets, cycle_strength, block_tile):
    per_block = cycle_cells.shape[1] // block_tile.shape[0]
    cycle_tile = jnp.repeat(block_tile, per_block)
    cell_r = jnp.clip(cycle_tile % N_COL * CR + cycle_cells[0], 16, NR - 3).astype(jnp.int32)
    cell_z = jnp.clip(cycle_tile // N_COL * CZ + cycle_cells[1], 2, NZ - 3).astype(jnp.int32)
    positions = jnp.stack([cell_r.astype(jnp.float32) + cycle_offsets[0], cell_z.astype(jnp.float32) + cycle_offsets[1]])
    sources = jnp.concatenate([positions, cycle_strength[None, :]], axis=0)
    velocity = cycle_velocity(positions, sources)
    displacement = STEP_LENGTH * velocity
    moved_offsets = jnp.clip(cycle_offsets + displacement, -1.0, 2.0)
    deposited = jnp.zeros((NR, NZ), jnp.float32)
    for lag_r in range(4):
        for lag_z in range(4):
            amount = cycle_strength * tent_weight(moved_offsets[0] - (lag_r - 1)) * tent_weight(moved_offsets[1] - (lag_z - 1))
            deposited = deposited.at[cell_r + (lag_r - 1), cell_z + (lag_z - 1)].add(amount)
    diffused = diffuse(jnp.pad(deposited, 1), 0)
    renewed = jnp.zeros(cycle_strength.shape, jnp.float32)
    for lag_r in range(4):
        for lag_z in range(4):
            weight = tent_weight(moved_offsets[0] - (lag_r - 1)) * tent_weight(moved_offsets[1] - (lag_z - 1))
            renewed = renewed + weight * diffused[cell_r + (lag_r - 1), cell_z + (lag_z - 1)]
    return (displacement, diffused, renewed)
```

```python
import jax
import jax.numpy as jnp
from jax import lax
from jax.experimental import pallas as pl
from jax.experimental.pallas import tpu as pltpu
from jax.sharding import PartitionSpec as P

MESH = pl.DeviceIdType.MESH
F32 = jnp.float32
BF16 = jnp.bfloat16
HIGH = lax.Precision.HIGHEST

N_ROW = 8
N_COL = 16
DEVICES = N_ROW * N_COL
CYC = 128
CR = 256
CZ = 1024
EXT_R = 264
EXT_Z = 1152
ROWS = 280
SLOTS = 512
VISCOSITY = 0.2
CORE_SQUARE = 4.0
STEP_LENGTH = 4.0
CHUNK = 16


def iota(shape, dim):
    return lax.broadcasted_iota(jnp.int32, shape, dim)


def dot(a, b, contract, precision=None):
    return lax.dot_general(
        a, b, (contract, ((), ())), precision=precision, preferred_element_type=F32
    )


def halves(x):
    high = x.astype(BF16)
    return high, (x - high.astype(F32)).astype(BF16)


def dot3(a, b, contract):
    (ah, al), (bh, bl) = a, b
    return dot(ah, bh, contract) + (dot(ah, bl, contract) + dot(al, bh, contract))


def tent(x):
    return jnp.maximum(1.0 - jnp.abs(x), 0.0)


def pair_terms(r, rr, z, a, a2, aa, src_z):
    d = z - src_z
    gap = a - r
    s = d * d + CORE_SQUARE
    near = s + gap * gap
    w = a2 * r
    u = near + w
    pq = (u + w) * near
    g = pq * lax.rsqrt(pq)
    b = g * lax.rsqrt(g)
    x = (u + g) * 0.5
    a = x * lax.rsqrt(x)
    t = []
    for _ in range(4):
        product = a * b
        t.append(product)
        a = (a + b) * 0.5
        b = product * lax.rsqrt(product)
    twice = a + b
    h = t[3]
    for n in (2, 1, 0):
        h = (h + h) + t[n]
    e = (8.0 * twice) * twice - ((h + h) + g)
    inverse = 1.0 / twice
    y = (e * inverse) * (1.0 / pq)
    radial = (u * y - inverse) * d
    even = inverse - y * s
    odd = y * (aa - rr)
    return radial, even + odd, even - odd


def kernel(
    cells_ref, offs_ref, stren_ref, btile_ref,
    disp_ref, diff_ref, renew_ref,
    src, ag, ret_send, ret_recv, tr, tz, tg, trr, acc_rad, acc_ax,
    out1, in1, out2, in2, rv, zf, zh, zl, ns_send, ns_recv, ew_send, ew_recv, co_recv, dep, fld,
    ag_ssem, ag_rsem, ret_sem, a1_sem, halo_ssem, halo_rsem, a2_sem,
):
    row = lax.axis_index("row")
    col = lax.axis_index("col")

    def at(kr, kc):
        return lax.rem(row + kr, N_ROW), lax.rem(col + kc, N_COL)

    def before(kr, kc):
        return lax.rem(row + (N_ROW - kr), N_ROW), lax.rem(col + (N_COL - kc), N_COL)

    def each_shift(body):
        def first(i, carry):
            body(0, 1 + i, True)
            return carry

        def middle(i, carry):
            body(1 + i // N_COL, lax.rem(i, N_COL), True)
            return carry

        def last(i, carry):
            body(4, 1 + i, True)
            return carry

        def alone(i, carry):
            body(4 * lax.rem(i, 2), 8 * (1 - i // 2), False)
            return carry

        lax.fori_loop(0, 7, first, 0)
        lax.fori_loop(0, 48, middle, 0)
        lax.fori_loop(0, 7, last, 0)
        lax.fori_loop(0, 2, alone, 0)
        body(4, 0, False)

    barrier = pltpu.get_barrier_semaphore()

    def greet(kr, kc, _):
        pl.semaphore_signal(barrier, inc=1, device_id=at(kr, kc), device_id_type=MESH)

    each_shift(greet)

    widen = (iota((64, CYC), 1) // 2 == iota((64, CYC), 0)).astype(F32)
    tile_of = dot(
        jnp.broadcast_to(btile_ref[...].astype(F32), (8, 64)), widen, ((1,), (0,)), HIGH
    )[0:1]
    tile_row = tile_of.astype(jnp.int32)
    part = tile_row & (N_COL - 1)
    slab = tile_row >> 4
    cell_r = jnp.clip(part * CR + cells_ref[0:1], 16, CR * N_COL - 3)
    cell_z = jnp.clip(slab * CZ + cells_ref[1:2], 2, CZ * N_ROW - 3)
    offs = offs_ref[...]
    pos_r = cell_r.astype(F32) + offs[0:1]
    pos_z = cell_z.astype(F32) + offs[1:2]
    strength = stren_ref[...]
    src[0:1] = pos_r
    src[1:2] = pos_z
    src[2:3] = (STEP_LENGTH * 0.5) * strength
    src[3:4] = jnp.zeros((1, CYC), F32)

    pl.semaphore_wait(barrier, 65)

    def send_source(kr, kc, _):
        pltpu.make_async_remote_copy(
            src_ref=src,
            dst_ref=ag.at[kr, kc],
            send_sem=ag_ssem,
            recv_sem=ag_rsem.at[kr, kc],
            device_id=before(kr, kc),
            device_id_type=MESH,
        ).start()

    each_shift(send_source)

    def column(v):
        return jnp.transpose(jnp.broadcast_to(v, (CYC, CYC)))

    tr[...] = column(pos_r)
    tz[...] = column(pos_z)
    tg[...] = column((STEP_LENGTH * 0.5) * strength)
    trr[...] = tr[...] * tr[...]
    acc_rad[...] = jnp.zeros((CYC, CYC), F32)
    acc_ax[...] = jnp.zeros((CYC, CYC), F32)

    def block(ref):
        a = ref[0:1, :]
        src_z = ref[1:2, :]
        src_g = ref[2:3, :]
        a, a2, aa, src_z, src_g = (
            jnp.broadcast_to(v, (CHUNK, CYC)) for v in (a, a + a, a * a, src_z, src_g)
        )
        back_rad = jnp.zeros((CHUNK, CYC), F32)
        back_ax = jnp.zeros((CHUNK, CYC), F32)
        for i in range(CYC // CHUNK):
            rows = pl.ds(i * CHUNK, CHUNK)
            radial, here, there = pair_terms(tr[rows], trr[rows], tz[rows], a, a2, aa, src_z)
            acc_rad[rows] += radial * src_g
            acc_ax[rows] += here * src_g
            own = tg[rows]
            back_rad += radial * own
            back_ax += there * own
        return back_rad, back_ax

    block(src)

    def meet(kr, kc, both):
        pltpu.make_async_copy(src, ag.at[kr, kc], ag_rsem.at[kr, kc]).wait()
        back_rad, back_ax = block(ag.at[kr, kc])
        if both:
            ret_send[kr, kc, 0:1] = jnp.sum(back_rad, axis=0, keepdims=True)
            ret_send[kr, kc, 1:2] = jnp.sum(back_ax, axis=0, keepdims=True)
            pltpu.make_async_remote_copy(
                src_ref=ret_send.at[kr, kc],
                dst_ref=ret_recv.at[kr, kc],
                send_sem=ret_sem.at[0],
                recv_sem=ret_sem.at[1],
                device_id=at(kr, kc),
                device_id_type=MESH,
            ).start()

    each_shift(meet)

    def wait_bytes(ref, count, sem):
        view = ref.at[pl.ds(0, count)]
        pltpu.make_async_copy(view, view, sem).wait()

    lane = iota((CYC, CYC), 1)
    sub = iota((CYC, CYC), 0)
    tile_rows = jnp.broadcast_to(tile_of, (CYC, CYC))
    same = (jnp.transpose(tile_rows) == tile_rows) & ((sub >> 1) < (lane >> 1))
    rank = jnp.sum(same.astype(F32), axis=0, keepdims=True)
    slot = rank.astype(jnp.int32) + (iota((1, CYC), 1) & 1)
    route = (sub == jnp.broadcast_to(tile_row, (CYC, CYC))).astype(F32)

    own_rad = jnp.sum(jnp.transpose(acc_rad[...]), axis=0, keepdims=True)
    own_ax = jnp.sum(jnp.transpose(acc_ax[...]), axis=0, keepdims=True)

    flat = ret_recv.reshape(5 * N_COL, 2, CYC)
    wait_bytes(flat, 62, ret_sem.at[1])
    got = jnp.sum(ret_recv[1:4], axis=(0, 1))
    got += jnp.sum(ret_recv[0, 1:8], axis=0) + jnp.sum(ret_recv[4, 1:8], axis=0)
    disp_r = (own_rad - got[0:1]) / pos_r
    disp_z = own_ax + got[1:2]
    disp_ref[0:1] = disp_r
    disp_ref[1:2] = disp_z

    moved_r = jnp.clip(offs[0:1] + disp_r, -1.0, 2.0)
    moved_z = jnp.clip(offs[1:2] + disp_z, -1.0, 2.0)
    local_r = (cell_r - part * CR).astype(F32)
    local_z = (cell_z - slab * CZ).astype(F32)
    blank = jnp.zeros((3, CYC), F32)
    values = jnp.concatenate([local_r, moved_r, local_z, moved_z, strength, blank], axis=0)
    payload = jnp.concatenate([jnp.where(slot == s, values, 0.0) for s in range(4)], axis=0)
    payload = jnp.concatenate([payload, jnp.zeros((96, CYC), F32)], axis=0)
    out1[:, 0, :] = dot(route, payload, ((1,), (1,)), HIGH)

    me = row * N_COL + col

    def to_all(out, into, sem):
        def outer(kr, carry):
            dr = lax.rem(row + kr, N_ROW)

            def send(dc):
                pltpu.make_async_remote_copy(
                    src_ref=out.at[dr * N_COL + dc],
                    dst_ref=into.at[me],
                    send_sem=sem.at[0],
                    recv_sem=sem.at[1],
                    device_id=(dr, dc),
                    device_id_type=MESH,
                ).start()

            for kc in range(1, N_COL):
                send(lax.rem(col + kc, N_COL))

            @pl.when(kr > 0)
            def _():
                send(col)

            return carry

        lax.fori_loop(0, N_ROW, outer, 0)
        into[me] = out[me]
        wait_bytes(into, DEVICES - 1, sem.at[1])

    to_all(out1, in1, a1_sem)

    rv[...] = in1[:, 0, :]
    across = jnp.transpose(rv[...])
    step = iota((ROWS, CYC), 0)
    wrapped = (iota((ROWS, CYC), 0) & 7) - jnp.where((iota((ROWS, CYC), 0) & 7) < 4, 0, 8)
    cell_of_row = jnp.where(
        step < 260,
        step,
        jnp.where(step < 264, step - 264, jnp.where(step < 272, CR + wrapped, wrapped)),
    ).astype(F32)
    radial = []
    for s in range(4):
        radial.append(tent((cell_of_row - across[8 * s : 8 * s + 1]) - across[8 * s + 1 : 8 * s + 2]))
    radial = jnp.concatenate(radial, axis=1)
    power = jnp.concatenate([across[8 * s + 4 : 8 * s + 5] for s in range(4)], axis=1)
    loaded = halves(radial * power)

    edge = iota((16, CYC), 0) & 7
    edge = edge - jnp.where(edge < 4, 0, 8) + jnp.where(iota((16, CYC), 0) < 8, CZ, 0)
    edge = edge.astype(F32)
    axial_edge = jnp.concatenate(
        [
            tent((edge - across[8 * s + 2 : 8 * s + 3]) - across[8 * s + 3 : 8 * s + 4])
            for s in range(4)
        ],
        axis=1,
    )
    strips = dot3(halves(axial_edge), loaded, ((1,), (1,)))
    ew_send[...] = jnp.zeros((2, 8, 384), F32)
    ew_send[0, :, 0:ROWS] = strips[0:8]
    ew_send[1, :, 0:ROWS] = strips[8:16]

    next_r, prev_r = lax.rem(row + 1, N_ROW), lax.rem(row + N_ROW - 1, N_ROW)
    next_c, prev_c = lax.rem(col + 1, N_COL), lax.rem(col + N_COL - 1, N_COL)
    copies = []

    def give(source, target, device):
        i = len(copies)
        copy = pltpu.make_async_remote_copy(
            src_ref=source,
            dst_ref=target,
            send_sem=halo_ssem.at[i],
            recv_sem=halo_rsem.at[i],
            device_id=device,
            device_id_type=MESH,
        )
        copy.start()
        copies.append(copy)

    give(ew_send.at[0], ew_recv.at[0], (next_r, col))
    give(ew_send.at[1], ew_recv.at[1], (prev_r, col))
    give(ew_send.at[0, :, pl.ds(256, 128)], co_recv.at[0], (next_r, next_c))
    give(ew_send.at[0, :, pl.ds(256, 128)], co_recv.at[1], (next_r, prev_c))
    give(ew_send.at[1, :, pl.ds(256, 128)], co_recv.at[2], (prev_r, next_c))
    give(ew_send.at[1, :, pl.ds(256, 128)], co_recv.at[3], (prev_r, prev_c))

    cell_of_lane = iota((16, EXT_Z), 1)
    cell_of_lane = jnp.where(cell_of_lane < 1088, cell_of_lane, cell_of_lane - EXT_Z).astype(F32)

    for s in range(4):

        def axial(i, carry):
            rows = pl.ds(pl.multiple_of(i * 16, 16), 16)
            into = pl.ds(pl.multiple_of(s * CYC + i * 16, 16), 16)
            one = rv[rows, :]
            w = tent((cell_of_lane - one[:, 8 * s + 2 : 8 * s + 3]) - one[:, 8 * s + 3 : 8 * s + 4])
            high, low = halves(w)
            zh[into] = high
            zl[into] = low
            return carry

        lax.fori_loop(0, 8, axial, 0)

    loaded_h, loaded_l = loaded
    along = ((1,), (0,))
    ends = dot3((loaded_h[EXT_R:], loaded_l[EXT_R:]), (zh[...], zl[...]), along)
    ns_send[0] = ends[0:8]
    ns_send[1] = ends[8:16]
    give(ns_send.at[0], ns_recv.at[0], (row, next_c))
    give(ns_send.at[1], ns_recv.at[1], (row, prev_c))

    dep[...] = dot3((loaded_h[:EXT_R], loaded_l[:EXT_R]), (zh[...], zl[...]), along)

    for copy in copies:
        copy.wait_recv()

    has_next_r, has_prev_r = row < N_ROW - 1, row > 0
    has_next_c, has_prev_c = col < N_COL - 1, col > 0
    strip_lane = iota((8, CYC), 1)

    def side(i, present):
        wide = jnp.where(present, ew_recv[i], 0.0)
        first, second, third = wide[:, 0:128], wide[:, 128:256], wide[:, 256:384]
        third = jnp.where(strip_lane < 8, third, 0.0)
        low = jnp.where(has_prev_c & present, pltpu.roll(co_recv[2 * i], 120, axis=1), 0.0)
        high = jnp.where(has_next_c & present, co_recv[2 * i + 1], 0.0)
        first += jnp.where(strip_lane < 4, low, 0.0)
        third += jnp.where((strip_lane >= 4) & (strip_lane < 8), low, 0.0)
        third += jnp.where(strip_lane < 4, pltpu.roll(high, 112, axis=1), 0.0)
        second += jnp.where(strip_lane >= 124, pltpu.roll(high, 104, axis=1), 0.0)
        wide = jnp.concatenate([first, second, third], axis=1)
        upper = iota((8, 384), 0) < 4
        wide = jnp.concatenate(
            [jnp.where(upper, wide, 0.0), jnp.zeros((112, 384), F32), jnp.where(upper, 0.0, wide)],
            axis=0,
        )
        return jnp.transpose(wide)[0:EXT_R]

    left = side(0, has_prev_r)
    right = side(1, has_next_r)
    front = iota((EXT_R, 128), 1) < 64
    dep[:, 0:128] += jnp.where(front, left, 0.0)
    dep[:, 896:1024] += jnp.where(front, 0.0, right)
    dep[:, 1024:1152] += jnp.where(front, right, left)
    upper = iota((8, EXT_Z), 0) < 4
    above = jnp.where(has_prev_c, ns_recv[0], 0.0)
    below = jnp.where(has_next_c, ns_recv[1], 0.0)
    dep[0:8] += jnp.where(upper, above, 0.0)
    dep[248:256] += jnp.where(upper, 0.0, below)
    dep[256:264] += jnp.where(upper, below, above)

    base = col * CR
    for i in range(EXT_R // 8):
        here = dep[8 * i : 8 * i + 8]
        prev = dep[8 * i - 8 : 8 * i] if i else dep[EXT_R - 8 : EXT_R]
        nxt = dep[8 * i + 8 : 8 * i + 16] if i < EXT_R // 8 - 1 else dep[0:8]
        inward = jnp.concatenate([prev[7:8], here[0:7]], axis=0)
        outward = jnp.concatenate([here[1:8], nxt[0:1]], axis=0)
        forward = pltpu.roll(here, EXT_Z - 1, axis=1)
        backward = pltpu.roll(here, 1, axis=1)
        number = iota((8, 128), 0) + 8 * i
        number = jnp.where(number < 260, number, number - EXT_R) + base
        radius = jnp.maximum(number, 1).astype(F32)
        half = jnp.concatenate([0.5 / radius] * 9, axis=1)
        square = jnp.concatenate([1.0 / (radius * radius)] * 9, axis=1)
        laplace = (
            (outward + inward)
            + (forward + backward)
            - 4.0 * here
            + (outward - inward) * half
            - here * square
        )
        new = here + VISCOSITY * laplace
        fld[8 * i : 8 * i + 8] = new
        if i < CR // 8:
            diff_ref[8 * i : 8 * i + 8] = new[:, 0:CZ]

    read = dot3(halves(fld[...]), (zh[...], zl[...]), ((1,), (1,)))
    found = jnp.sum(read * radial[:EXT_R], axis=0, keepdims=True)
    found = jnp.concatenate(
        [found[:, CYC * s : CYC * s + CYC] for s in range(4)] + [jnp.zeros((124, CYC), F32)], axis=0
    )
    out2[:, 0, :] = jnp.transpose(found)
    to_all(out2, in2, a2_sem)
    table = jnp.transpose(in2[:, 0, :])[0:8]
    mine = dot(table, route, ((1,), (0,)), HIGH)
    renew_ref[...] = jnp.sum(
        jnp.where(iota((8, CYC), 0) == slot, mine, 0.0), axis=0, keepdims=True
    )

    sent = ag.reshape(5 * N_COL, 4, CYC)
    wait_bytes(sent, 65, ag_ssem)
    wait_bytes(flat, 62, ret_sem.at[0])
    wait_bytes(out1, DEVICES - 1, a1_sem.at[0])
    wait_bytes(out2, DEVICES - 1, a2_sem.at[0])
    for copy in copies:
        copy.wait_send()


def on_device(cycle_cells, cycle_offsets, cycle_strength, block_tile):
    vmem = pl.BlockSpec(memory_space=pltpu.VMEM)
    dma = pltpu.SemaphoreType.DMA
    displacement, diffused, renewed = pl.pallas_call(
        kernel,
        out_shape=[
            jax.ShapeDtypeStruct((2, CYC), F32),
            jax.ShapeDtypeStruct((CR, CZ), F32),
            jax.ShapeDtypeStruct((1, CYC), F32),
        ],
        in_specs=[vmem] * 4,
        out_specs=[vmem] * 3,
        scratch_shapes=[
            pltpu.VMEM((4, CYC), F32),
            pltpu.VMEM((5, N_COL, 4, CYC), F32),
            pltpu.VMEM((5, N_COL, 2, CYC), F32),
            pltpu.VMEM((5, N_COL, 2, CYC), F32),
            pltpu.VMEM((CYC, CYC), F32),
            pltpu.VMEM((CYC, CYC), F32),
            pltpu.VMEM((CYC, CYC), F32),
            pltpu.VMEM((CYC, CYC), F32),
            pltpu.VMEM((CYC, CYC), F32),
            pltpu.VMEM((CYC, CYC), F32),
            pltpu.VMEM((DEVICES, 1, CYC), F32),
            pltpu.VMEM((DEVICES, 1, CYC), F32),
            pltpu.VMEM((DEVICES, 1, CYC), F32),
            pltpu.VMEM((DEVICES, 1, CYC), F32),
            pltpu.VMEM((CYC, CYC), F32),
            pltpu.VMEM((8, 128), F32),
            pltpu.VMEM((SLOTS, EXT_Z), BF16),
            pltpu.VMEM((SLOTS, EXT_Z), BF16),
            pltpu.VMEM((2, 8, EXT_Z), F32),
            pltpu.VMEM((2, 8, EXT_Z), F32),
            pltpu.VMEM((2, 8, 384), F32),
            pltpu.VMEM((2, 8, 384), F32),
            pltpu.VMEM((4, 8, 128), F32),
            pltpu.VMEM((EXT_R, EXT_Z), F32),
            pltpu.VMEM((EXT_R, EXT_Z), F32),
            dma,
            dma((5, N_COL)),
            dma((2,)),
            dma((2,)),
            dma((8,)),
            dma((8,)),
            dma((2,)),
        ],
        compiler_params=pltpu.CompilerParams(
            collective_id=0, has_side_effects=True, vmem_limit_bytes=48 * 2**20
        ),
    )(cycle_cells, cycle_offsets, cycle_strength.reshape(1, CYC), block_tile.reshape(1, -1))
    return displacement, diffused, renewed.reshape(CYC)


def solution(mesh):
    in_specs = (
        P(None, ("row", "col")),
        P(None, ("row", "col")),
        P(("row", "col")),
        P(("row", "col")),
    )
    out_specs = (P(None, ("row", "col")), P("col", "row"), P(("row", "col")))
    return jax.shard_map(
        on_device, mesh=mesh, in_specs=in_specs, out_specs=out_specs, check_vma=False
    )
```

```python
import jax
import jax.numpy as jnp
from jax import lax
from jax.experimental import pallas as pl
from jax.experimental.pallas import tpu as pltpu
from jax.sharding import PartitionSpec as P

MESH = pl.DeviceIdType.MESH
F32 = jnp.float32
BF16 = jnp.bfloat16
HIGH = lax.Precision.HIGHEST

N_ROW = 8
N_COL = 16
DEVICES = N_ROW * N_COL
CYC = 128
CR = 256
CZ = 1024
EXT_R = 264
EXT_Z = 1152
ROWS = 280
SLOTS = 512
VISCOSITY = 0.2
CORE_SQUARE = 4.0
STEP_LENGTH = 4.0
CHUNK = 128


def iota(shape, dim):
    return lax.broadcasted_iota(jnp.int32, shape, dim)


def dot(a, b, contract, precision=None):
    return lax.dot_general(
        a, b, (contract, ((), ())), precision=precision, preferred_element_type=F32
    )


def halves(x):
    high = x.astype(BF16)
    return high, (x - high.astype(F32)).astype(BF16)


def dot3(a, b, contract):
    (ah, al), (bh, bl) = a, b
    return dot(ah, bh, contract) + (dot(ah, bl, contract) + dot(al, bh, contract))


def tent(x):
    return jnp.maximum(1.0 - jnp.abs(x), 0.0)


def pair_terms(r, rr, z, a, a2, aa, src_z):
    d = z - src_z
    gap = a - r
    s = d * d + CORE_SQUARE
    near = s + gap * gap
    w = a2 * r
    u = near + w
    pq = (u + w) * near
    g = pq * lax.rsqrt(pq)
    b = g * lax.rsqrt(g)
    x = (u + g) * 0.5
    a = x * lax.rsqrt(x)
    t = []
    for _ in range(4):
        product = a * b
        t.append(product)
        a = (a + b) * 0.5
        b = product * lax.rsqrt(product)
    twice = a + b
    h = t[3]
    for n in (2, 1, 0):
        h = (h + h) + t[n]
    e = (8.0 * twice) * twice - ((h + h) + g)
    inverse = 1.0 / twice
    y = (e * inverse) * (1.0 / pq)
    radial = (u * y - inverse) * d
    even = inverse - y * s
    odd = y * (aa - rr)
    return radial, even + odd, even - odd


def kernel(
    cells_hbm, offs_hbm, stren_hbm, btile_hbm,
    disp_out, diff_out, renew_out,
    cells_ref, offs_ref, stren_ref, btile_ref, disp_ref, renew_ref,
    src, ag, ret_send, ret_recv, tr, tz, tg, trr, acc_rad, acc_ax,
    out1, in1, out2, in2, rv, zh, zl, ns_send, ns_recv, ew_send, ew_recv, co_recv, dep, fld,
    load_sem, store_sem, ag_ssem, ag_rsem, ret_sem, a1_sem, halo_ssem, halo_rsem, a2_sem,
):
    row = lax.axis_index("row")
    col = lax.axis_index("col")

    def at(kr, kc):
        return lax.rem(row + kr, N_ROW), lax.rem(col + kc, N_COL)

    def before(kr, kc):
        return lax.rem(row + (N_ROW - kr), N_ROW), lax.rem(col + (N_COL - kc), N_COL)

    segments = [
        (4, lambda i: 0, lambda i: 4 + i, True),
        (8, lambda i: 2, lambda i: i, True),
        (7, lambda i: 4, lambda i: 1 + i, True),
        (32, lambda i: 3 - 2 * (i // N_COL), lambda i: lax.rem(i, N_COL), True),
        (8, lambda i: 2, lambda i: 8 + i, True),
        (3, lambda i: 0, lambda i: 3 - i, True),
        (3, lambda i: 4 * ((i + 1) // 2), lambda i: 8 * (1 - i // 2), False),
    ]

    def over(segment, body):
        count, kr, kc, _ = segment

        def one(i, carry):
            body(kr(i), kc(i))
            return carry

        lax.fori_loop(0, count, one, 0)

    def each_shift(body):
        for segment in segments:
            over(segment, body)

    loads = [
        pltpu.make_async_copy(source, target, load_sem.at[i])
        for i, (source, target) in enumerate(
            (
                (btile_hbm, btile_ref),
                (cells_hbm, cells_ref),
                (offs_hbm, offs_ref),
                (stren_hbm, stren_ref),
            )
        )
    ]
    for load in loads:
        load.start()
    barrier = pltpu.get_barrier_semaphore()

    def greet(kr, kc):
        pl.semaphore_signal(barrier, inc=1, device_id=at(kr, kc), device_id_type=MESH)

    each_shift(greet)

    for load in loads:
        load.wait()
    widen = (iota((64, CYC), 1) // 2 == iota((64, CYC), 0)).astype(F32)
    tile_of = dot(
        jnp.broadcast_to(btile_ref[...].astype(F32), (8, 64)), widen, ((1,), (0,)), HIGH
    )[0:1]
    tile_row = tile_of.astype(jnp.int32)
    part = tile_row & (N_COL - 1)
    slab = tile_row >> 4
    cell_r = jnp.clip(part * CR + cells_ref[0:1], 16, CR * N_COL - 3)
    cell_z = jnp.clip(slab * CZ + cells_ref[1:2], 2, CZ * N_ROW - 3)
    offs = offs_ref[...]
    pos_r = cell_r.astype(F32) + offs[0:1]
    pos_z = cell_z.astype(F32) + offs[1:2]
    strength = stren_ref[...]
    src[0:1] = pos_r
    src[1:2] = pos_z
    src[2:3] = (STEP_LENGTH * 0.5) * strength
    src[3:4] = jnp.zeros((1, CYC), F32)

    def column(v):
        return jnp.transpose(jnp.broadcast_to(v, (CYC, CYC)))

    tr[...] = column(pos_r)
    tz[...] = column(pos_z)
    tg[...] = column((STEP_LENGTH * 0.5) * strength)
    trr[...] = tr[...] * tr[...]
    acc_rad[...] = jnp.zeros((CYC, CYC), F32)
    acc_ax[...] = jnp.zeros((CYC, CYC), F32)

    def block(ref):
        a = ref[0:1, :]
        src_z = ref[1:2, :]
        src_g = ref[2:3, :]
        a, a2, aa, src_z, src_g = (
            jnp.broadcast_to(v, (CHUNK, CYC)) for v in (a, a + a, a * a, src_z, src_g)
        )
        back_rad = jnp.zeros((CHUNK, CYC), F32)
        back_ax = jnp.zeros((CHUNK, CYC), F32)
        for i in range(CYC // CHUNK):
            rows = pl.ds(i * CHUNK, CHUNK)
            radial, here, there = pair_terms(tr[rows], trr[rows], tz[rows], a, a2, aa, src_z)
            acc_rad[rows] += radial * src_g
            acc_ax[rows] += here * src_g
            own = tg[rows]
            back_rad += radial * own
            back_ax += there * own
        return back_rad, back_ax

    block(src)

    lane = iota((CYC, CYC), 1)
    sub = iota((CYC, CYC), 0)
    tile_rows = jnp.broadcast_to(tile_of, (CYC, CYC))
    same = (jnp.transpose(tile_rows) == tile_rows) & ((sub >> 1) < (lane >> 1))
    rank = jnp.sum(same.astype(F32), axis=0, keepdims=True)
    slot = rank.astype(jnp.int32) + (iota((1, CYC), 1) & 1)
    route = (sub == jnp.broadcast_to(tile_row, (CYC, CYC))).astype(F32)

    pl.semaphore_wait(barrier, 65)

    def send_source(kr, kc):
        pltpu.make_async_remote_copy(
            src_ref=src,
            dst_ref=ag.at[kr, kc],
            send_sem=ag_ssem,
            recv_sem=ag_rsem.at[kr, kc],
            device_id=before(kr, kc),
            device_id_type=MESH,
        ).start()

    each_shift(send_source)

    def arrive(kr, kc):
        pltpu.make_async_copy(src, ag.at[kr, kc], ag_rsem.at[kr, kc]).wait()

    def meet(kr, kc):
        back_rad, back_ax = block(ag.at[kr, kc])
        ret_send[kr, kc, 0:1] = jnp.sum(back_rad, axis=0, keepdims=True)
        ret_send[kr, kc, 1:2] = jnp.sum(back_ax, axis=0, keepdims=True)

    def send_back(kr, kc):
        pltpu.make_async_remote_copy(
            src_ref=ret_send.at[kr, kc],
            dst_ref=ret_recv.at[kr, kc],
            send_sem=ret_sem.at[0],
            recv_sem=ret_sem.at[1],
            device_id=at(kr, kc),
            device_id_type=MESH,
        ).start()

    def arrive_meet(kr, kc):
        arrive(kr, kc)
        meet(kr, kc)

    def full_meet(kr, kc):
        arrive_meet(kr, kc)
        send_back(kr, kc)

    for segment in segments:
        over(segment, full_meet if segment[-1] else arrive_meet)

    def wait_bytes(ref, count, sem):
        view = ref.at[pl.ds(0, count)]
        pltpu.make_async_copy(view, view, sem).wait()

    own_rad = jnp.sum(jnp.transpose(acc_rad[...]), axis=0, keepdims=True)
    own_ax = jnp.sum(jnp.transpose(acc_ax[...]), axis=0, keepdims=True)

    flat = ret_recv.reshape(5 * N_COL, 2, CYC)
    wait_bytes(flat, 62, ret_sem.at[1])
    got = jnp.sum(ret_recv[1:4], axis=(0, 1))
    got += jnp.sum(ret_recv[0, 1:8], axis=0) + jnp.sum(ret_recv[4, 1:8], axis=0)
    disp_r = (own_rad - got[0:1]) / pos_r
    disp_z = own_ax + got[1:2]
    disp_ref[0:1] = disp_r
    disp_ref[1:2] = disp_z
    stores = [pltpu.make_async_copy(disp_ref, disp_out, store_sem.at[0])]
    stores[0].start()

    moved_r = jnp.clip(offs[0:1] + disp_r, -1.0, 2.0)
    moved_z = jnp.clip(offs[1:2] + disp_z, -1.0, 2.0)
    local_r = (cell_r - part * CR).astype(F32)
    local_z = (cell_z - slab * CZ).astype(F32)
    blank = jnp.zeros((3, CYC), F32)
    values = jnp.concatenate([local_r, moved_r, local_z, moved_z, strength, blank], axis=0)
    payload = jnp.concatenate([jnp.where(slot == s, values, 0.0) for s in range(4)], axis=0)
    payload = jnp.concatenate([payload, jnp.zeros((96, CYC), F32)], axis=0)
    out1[:, 0, :] = dot(route, payload, ((1,), (1,)), HIGH)

    me = row * N_COL + col

    def to_all(out, into, sem):
        def outer(i, carry):
            kr = lax.rem(3 * i + 3, N_ROW)
            dr = lax.rem(row + kr, N_ROW)

            def send(dc):
                pltpu.make_async_remote_copy(
                    src_ref=out.at[dr * N_COL + dc],
                    dst_ref=into.at[me],
                    send_sem=sem.at[0],
                    recv_sem=sem.at[1],
                    device_id=(dr, dc),
                    device_id_type=MESH,
                ).start()

            for kc in range(1, N_COL):
                send(lax.rem(col + kc, N_COL))

            @pl.when(kr > 0)
            def _():
                send(col)

            return carry

        lax.fori_loop(0, N_ROW, outer, 0)
        into[me] = out[me]
        wait_bytes(into, DEVICES - 1, sem.at[1])

    to_all(out1, in1, a1_sem)

    rv[...] = in1[:, 0, :]
    across = jnp.transpose(rv[...])
    step = iota((ROWS, CYC), 0)
    wrapped = (iota((ROWS, CYC), 0) & 7) - jnp.where((iota((ROWS, CYC), 0) & 7) < 4, 0, 8)
    cell_of_row = jnp.where(
        step < 260,
        step,
        jnp.where(step < 264, step - 264, jnp.where(step < 272, CR + wrapped, wrapped)),
    ).astype(F32)
    radial = []
    for s in range(4):
        radial.append(tent((cell_of_row - across[8 * s : 8 * s + 1]) - across[8 * s + 1 : 8 * s + 2]))
    radial = jnp.concatenate(radial, axis=1)
    power = jnp.concatenate([across[8 * s + 4 : 8 * s + 5] for s in range(4)], axis=1)
    loaded = halves(radial * power)

    edge = iota((16, CYC), 0) & 7
    edge = edge - jnp.where(edge < 4, 0, 8) + jnp.where(iota((16, CYC), 0) < 8, CZ, 0)
    edge = edge.astype(F32)
    axial_edge = jnp.concatenate(
        [
            tent((edge - across[8 * s + 2 : 8 * s + 3]) - across[8 * s + 3 : 8 * s + 4])
            for s in range(4)
        ],
        axis=1,
    )
    strips = dot3(halves(axial_edge), loaded, ((1,), (1,)))
    ew_send[...] = jnp.zeros((2, 8, 384), F32)
    ew_send[0, :, 0:ROWS] = strips[0:8]
    ew_send[1, :, 0:ROWS] = strips[8:16]

    next_r, prev_r = lax.rem(row + 1, N_ROW), lax.rem(row + N_ROW - 1, N_ROW)
    next_c, prev_c = lax.rem(col + 1, N_COL), lax.rem(col + N_COL - 1, N_COL)
    copies = []

    def give(source, target, device):
        i = len(copies)
        copy = pltpu.make_async_remote_copy(
            src_ref=source,
            dst_ref=target,
            send_sem=halo_ssem.at[i],
            recv_sem=halo_rsem.at[i],
            device_id=device,
            device_id_type=MESH,
        )
        copy.start()
        copies.append(copy)

    give(ew_send.at[0], ew_recv.at[0], (next_r, col))
    give(ew_send.at[1], ew_recv.at[1], (prev_r, col))
    give(ew_send.at[0, :, pl.ds(256, 128)], co_recv.at[0], (next_r, next_c))
    give(ew_send.at[0, :, pl.ds(256, 128)], co_recv.at[1], (next_r, prev_c))
    give(ew_send.at[1, :, pl.ds(256, 128)], co_recv.at[2], (prev_r, next_c))
    give(ew_send.at[1, :, pl.ds(256, 128)], co_recv.at[3], (prev_r, prev_c))

    cell_of_lane = iota((16, EXT_Z), 1)
    cell_of_lane = jnp.where(cell_of_lane < 1088, cell_of_lane, cell_of_lane - EXT_Z).astype(F32)

    for s in range(4):

        def axial(i, carry):
            rows = pl.ds(pl.multiple_of(i * 16, 16), 16)
            into = pl.ds(pl.multiple_of(s * CYC + i * 16, 16), 16)
            one = rv[rows, :]
            w = tent((cell_of_lane - one[:, 8 * s + 2 : 8 * s + 3]) - one[:, 8 * s + 3 : 8 * s + 4])
            high, low = halves(w)
            zh[into] = high
            zl[into] = low
            return carry

        lax.fori_loop(0, 8, axial, 0)

    loaded_h, loaded_l = loaded
    along = ((1,), (0,))
    ends = dot3((loaded_h[EXT_R:], loaded_l[EXT_R:]), (zh[...], zl[...]), along)
    ns_send[0] = ends[0:8]
    ns_send[1] = ends[8:16]
    give(ns_send.at[0], ns_recv.at[0], (row, next_c))
    give(ns_send.at[1], ns_recv.at[1], (row, prev_c))

    dep[...] = dot3((loaded_h[:EXT_R], loaded_l[:EXT_R]), (zh[...], zl[...]), along)

    for copy in copies:
        copy.wait_recv()

    has_next_r, has_prev_r = row < N_ROW - 1, row > 0
    has_next_c, has_prev_c = col < N_COL - 1, col > 0
    strip_lane = iota((8, CYC), 1)

    def side(i, present):
        wide = jnp.where(present, ew_recv[i], 0.0)
        first, second, third = wide[:, 0:128], wide[:, 128:256], wide[:, 256:384]
        third = jnp.where(strip_lane < 8, third, 0.0)
        low = jnp.where(has_prev_c & present, pltpu.roll(co_recv[2 * i], 120, axis=1), 0.0)
        high = jnp.where(has_next_c & present, co_recv[2 * i + 1], 0.0)
        first += jnp.where(strip_lane < 4, low, 0.0)
        third += jnp.where((strip_lane >= 4) & (strip_lane < 8), low, 0.0)
        third += jnp.where(strip_lane < 4, pltpu.roll(high, 112, axis=1), 0.0)
        second += jnp.where(strip_lane >= 124, pltpu.roll(high, 104, axis=1), 0.0)
        wide = jnp.concatenate([first, second, third], axis=1)
        upper = iota((8, 384), 0) < 4
        wide = jnp.concatenate(
            [jnp.where(upper, wide, 0.0), jnp.zeros((112, 384), F32), jnp.where(upper, 0.0, wide)],
            axis=0,
        )
        return jnp.transpose(wide)[0:EXT_R]

    left = side(0, has_prev_r)
    right = side(1, has_next_r)
    front = iota((EXT_R, 128), 1) < 64
    dep[:, 0:128] += jnp.where(front, left, 0.0)
    dep[:, 896:1024] += jnp.where(front, 0.0, right)
    dep[:, 1024:1152] += jnp.where(front, right, left)
    upper = iota((8, EXT_Z), 0) < 4
    above = jnp.where(has_prev_c, ns_recv[0], 0.0)
    below = jnp.where(has_next_c, ns_recv[1], 0.0)
    dep[0:8] += jnp.where(upper, above, 0.0)
    dep[248:256] += jnp.where(upper, 0.0, below)
    dep[256:264] += jnp.where(upper, below, above)

    base = col * CR
    for i in range(EXT_R // 8):
        here = dep[8 * i : 8 * i + 8]
        prev = dep[8 * i - 8 : 8 * i] if i else dep[EXT_R - 8 : EXT_R]
        nxt = dep[8 * i + 8 : 8 * i + 16] if i < EXT_R // 8 - 1 else dep[0:8]
        inward = jnp.concatenate([prev[7:8], here[0:7]], axis=0)
        outward = jnp.concatenate([here[1:8], nxt[0:1]], axis=0)
        forward = pltpu.roll(here, EXT_Z - 1, axis=1)
        backward = pltpu.roll(here, 1, axis=1)
        number = iota((8, 128), 0) + 8 * i
        number = jnp.where(number < 260, number, number - EXT_R) + base
        radius = jnp.maximum(number, 1).astype(F32)
        half = jnp.concatenate([0.5 / radius] * 9, axis=1)
        square = jnp.concatenate([1.0 / (radius * radius)] * 9, axis=1)
        laplace = (
            (outward + inward)
            + (forward + backward)
            - 4.0 * here
            + (outward - inward) * half
            - here * square
        )
        new = here + VISCOSITY * laplace
        fld[8 * i : 8 * i + 8] = new

    tile = fld.at[pl.ds(0, CR), pl.ds(0, CZ)]
    stores.append(pltpu.make_async_copy(tile, diff_out, store_sem.at[1]))
    stores[1].start()

    read = dot3(halves(fld[...]), (zh[...], zl[...]), ((1,), (1,)))
    found = jnp.sum(read * radial[:EXT_R], axis=0, keepdims=True)
    found = jnp.concatenate(
        [found[:, CYC * s : CYC * s + CYC] for s in range(4)] + [jnp.zeros((124, CYC), F32)], axis=0
    )
    out2[:, 0, :] = jnp.transpose(found)
    to_all(out2, in2, a2_sem)
    table = jnp.transpose(in2[:, 0, :])[0:8]
    mine = dot(table, route, ((1,), (0,)), HIGH)
    renew_ref[...] = jnp.sum(
        jnp.where(iota((8, CYC), 0) == slot, mine, 0.0), axis=0, keepdims=True
    )

    stores.append(pltpu.make_async_copy(renew_ref, renew_out, store_sem.at[2]))
    stores[2].start()

    sent = ag.reshape(5 * N_COL, 4, CYC)
    wait_bytes(sent, 65, ag_ssem)
    wait_bytes(flat, 62, ret_sem.at[0])
    wait_bytes(out1, DEVICES - 1, a1_sem.at[0])
    wait_bytes(out2, DEVICES - 1, a2_sem.at[0])
    for copy in copies:
        copy.wait_send()
    for store in stores:
        store.wait()


def write_out(disp_ref, diff_ref, renew_ref, disp_out, diff_out, renew_out, sem):
    pairs = [(disp_ref, disp_out), (renew_ref, renew_out)]
    for i in range(8):
        rows = pl.ds(i * CR // 8, CR // 8)
        pairs.append((diff_ref.at[rows], diff_out.at[rows]))
    copies = [
        pltpu.make_async_copy(source, target, sem.at[i])
        for i, (source, target) in enumerate(pairs)
    ]
    for copy in copies:
        copy.start()
    for copy in copies:
        copy.wait()


def on_device(cycle_cells, cycle_offsets, cycle_strength, block_tile):
    hbm = pl.BlockSpec(memory_space=pl.ANY)
    dma = pltpu.SemaphoreType.DMA
    shapes = [
        jax.ShapeDtypeStruct((2, CYC), F32),
        jax.ShapeDtypeStruct((CR, CZ), F32),
        jax.ShapeDtypeStruct((1, CYC), F32),
    ]
    results = pl.pallas_call(
        kernel,
        out_shape=shapes,
        in_specs=[hbm] * 4,
        out_specs=[hbm] * 3,
        scratch_shapes=[
            pltpu.VMEM((2, CYC), jnp.int32),
            pltpu.VMEM((2, CYC), F32),
            pltpu.VMEM((1, CYC), F32),
            pltpu.VMEM((1, 64), jnp.int32),
            pltpu.VMEM((2, CYC), F32),
            pltpu.VMEM((1, CYC), F32),
            pltpu.VMEM((4, CYC), F32),
            pltpu.VMEM((5, N_COL, 4, CYC), F32),
            pltpu.VMEM((5, N_COL, 2, CYC), F32),
            pltpu.VMEM((5, N_COL, 2, CYC), F32),
            pltpu.VMEM((CYC, CYC), F32),
            pltpu.VMEM((CYC, CYC), F32),
            pltpu.VMEM((CYC, CYC), F32),
            pltpu.VMEM((CYC, CYC), F32),
            pltpu.VMEM((CYC, CYC), F32),
            pltpu.VMEM((CYC, CYC), F32),
            pltpu.VMEM((DEVICES, 1, CYC), F32),
            pltpu.VMEM((DEVICES, 1, CYC), F32),
            pltpu.VMEM((DEVICES, 1, CYC), F32),
            pltpu.VMEM((DEVICES, 1, CYC), F32),
            pltpu.VMEM((CYC, CYC), F32),
            pltpu.VMEM((SLOTS, EXT_Z), BF16),
            pltpu.VMEM((SLOTS, EXT_Z), BF16),
            pltpu.VMEM((2, 8, EXT_Z), F32),
            pltpu.VMEM((2, 8, EXT_Z), F32),
            pltpu.VMEM((2, 8, 384), F32),
            pltpu.VMEM((2, 8, 384), F32),
            pltpu.VMEM((4, 8, 128), F32),
            pltpu.VMEM((EXT_R, EXT_Z), F32),
            pltpu.VMEM((EXT_R, EXT_Z), F32),
            dma((4,)),
            dma((3,)),
            dma,
            dma((5, N_COL)),
            dma((2,)),
            dma((2,)),
            dma((8,)),
            dma((8,)),
            dma((2,)),
        ],
        compiler_params=pltpu.CompilerParams(
            collective_id=0, has_side_effects=True, vmem_limit_bytes=40 * 2**20
        ),
    )(cycle_cells, cycle_offsets, cycle_strength.reshape(1, CYC), block_tile.reshape(1, -1))
    displacement, diffused, renewed = pl.pallas_call(
        write_out,
        out_shape=shapes,
        in_specs=[pl.BlockSpec(memory_space=pltpu.VMEM)] * 3,
        out_specs=[hbm] * 3,
        scratch_shapes=[dma((10,))],
        compiler_params=pltpu.CompilerParams(vmem_limit_bytes=2**20),
    )(*results)
    return displacement, diffused, renewed.reshape(CYC)


def solution(mesh):
    in_specs = (
        P(None, ("row", "col")),
        P(None, ("row", "col")),
        P(("row", "col")),
        P(("row", "col")),
    )
    out_specs = (P(None, ("row", "col")), P("col", "row"), P(("row", "col")))
    return jax.shard_map(
        on_device, mesh=mesh, in_specs=in_specs, out_specs=out_specs, check_vma=False
    )
```

```python
import jax
import jax.numpy as jnp
from jax import lax
from jax.experimental import pallas as pl
from jax.experimental.pallas import tpu as pltpu
from jax.sharding import PartitionSpec as P

MESH = pl.DeviceIdType.MESH
F32 = jnp.float32
BF16 = jnp.bfloat16
HIGH = lax.Precision.HIGHEST

N_ROW = 8
N_COL = 16
DEVICES = N_ROW * N_COL
CYC = 128
CR = 256
CZ = 1024
EXT_R = 264
EXT_Z = 1152
SLOTS = 512
VISCOSITY = 0.2
CORE_SQUARE = 4.0
STEP_LENGTH = 4.0
CHUNK = 128


def iota(shape, dim):
    return lax.broadcasted_iota(jnp.int32, shape, dim)


def dot(a, b, contract, precision=None):
    return lax.dot_general(
        a, b, (contract, ((), ())), precision=precision, preferred_element_type=F32
    )


def halves(x):
    high = x.astype(BF16)
    return high, (x - high.astype(F32)).astype(BF16)


def dot3(a, b, contract):
    (ah, al), (bh, bl) = a, b
    return dot(ah, bh, contract) + (dot(ah, bl, contract) + dot(al, bh, contract))


def tent(x):
    return jnp.maximum(1.0 - jnp.abs(x), 0.0)


def pair_terms(r, rr, z, a, a2, aa, src_z):
    d = z - src_z
    gap = a - r
    s = d * d + CORE_SQUARE
    near = s + gap * gap
    w = a2 * r
    u = near + w
    pq = (u + w) * near
    g = pq * lax.rsqrt(pq)
    b = g * lax.rsqrt(g)
    x = (u + g) * 0.5
    a = x * lax.rsqrt(x)
    t = []
    for _ in range(4):
        product = a * b
        t.append(product)
        a = (a + b) * 0.5
        b = product * lax.rsqrt(product)
    twice = a + b
    h = t[3]
    for n in (2, 1, 0):
        h = (h + h) + t[n]
    e = (8.0 * twice) * twice - ((h + h) + g)
    inverse = 1.0 / twice
    y = (e * inverse) * (1.0 / pq)
    radial = (u * y - inverse) * d
    even = inverse - y * s
    odd = y * (aa - rr)
    return radial, even + odd, even - odd


def kernel(
    cells_ref, offs_ref, stren_ref, btile_ref,
    disp_ref, diff_ref, renew_ref,
    src, ag, ret_send, ret_recv, tr, tz, tg, trr, acc_rad, acc_ax,
    out1, in1, out2, in2, zh, zl, ns_send, ns_recv, ew_send, ew_recv, co_send, co_recv, dep, fld,
    ag_ssem, ag_rsem, ret_sem, a1_sem, halo_ssem, halo_rsem, a2_sem,
):
    row = lax.axis_index("row")
    col = lax.axis_index("col")

    def at(kr, kc):
        return lax.rem(row + kr, N_ROW), lax.rem(col + kc, N_COL)

    def before(kr, kc):
        return lax.rem(row + (N_ROW - kr), N_ROW), lax.rem(col + (N_COL - kc), N_COL)

    segments = [
        (4, lambda i: 0, lambda i: 4 + i, True),
        (8, lambda i: 2, lambda i: i, True),
        (7, lambda i: 4, lambda i: 1 + i, True),
        (32, lambda i: 3 - 2 * (i // N_COL), lambda i: lax.rem(i, N_COL), True),
        (8, lambda i: 2, lambda i: 8 + i, True),
        (3, lambda i: 0, lambda i: 3 - i, True),
        (3, lambda i: 4 * ((i + 1) // 2), lambda i: 8 * (1 - i // 2), False),
    ]

    def over(segment, body):
        count, kr, kc, _ = segment

        def one(i, carry):
            body(kr(i), kc(i))
            return carry

        lax.fori_loop(0, count, one, 0)

    def each_shift(body):
        for segment in segments:
            over(segment, body)

    barrier = pltpu.get_barrier_semaphore()

    def greet(kr, kc):
        pl.semaphore_signal(barrier, inc=1, device_id=at(kr, kc), device_id_type=MESH)

    each_shift(greet)

    widen = (iota((64, CYC), 1) // 2 == iota((64, CYC), 0)).astype(F32)
    tile_of = dot(
        jnp.broadcast_to(btile_ref[...].astype(F32), (8, 64)), widen, ((1,), (0,)), HIGH
    )[0:1]
    tile_row = tile_of.astype(jnp.int32)
    part = tile_row & (N_COL - 1)
    slab = tile_row >> 4
    cell_r = jnp.clip(part * CR + cells_ref[0:1], 16, CR * N_COL - 3)
    cell_z = jnp.clip(slab * CZ + cells_ref[1:2], 2, CZ * N_ROW - 3)
    offs = offs_ref[...]
    pos_r = cell_r.astype(F32) + offs[0:1]
    pos_z = cell_z.astype(F32) + offs[1:2]
    strength = stren_ref[...]
    src[0:1] = pos_r
    src[1:2] = pos_z
    src[2:3] = (STEP_LENGTH * 0.5) * strength
    src[3:4] = jnp.zeros((1, CYC), F32)

    def column(v):
        return jnp.transpose(jnp.broadcast_to(v, (CYC, CYC)))

    tr[...] = column(pos_r)
    tz[...] = column(pos_z)
    tg[...] = column((STEP_LENGTH * 0.5) * strength)
    trr[...] = tr[...] * tr[...]
    acc_rad[...] = jnp.zeros((CYC, CYC), F32)
    acc_ax[...] = jnp.zeros((CYC, CYC), F32)

    def block(ref):
        a = ref[0:1, :]
        src_z = ref[1:2, :]
        src_g = ref[2:3, :]
        a, a2, aa, src_z, src_g = (
            jnp.broadcast_to(v, (CHUNK, CYC)) for v in (a, a + a, a * a, src_z, src_g)
        )
        back_rad = jnp.zeros((CHUNK, CYC), F32)
        back_ax = jnp.zeros((CHUNK, CYC), F32)
        for i in range(CYC // CHUNK):
            rows = pl.ds(i * CHUNK, CHUNK)
            radial, here, there = pair_terms(tr[rows], trr[rows], tz[rows], a, a2, aa, src_z)
            acc_rad[rows] += radial * src_g
            acc_ax[rows] += here * src_g
            own = tg[rows]
            back_rad += radial * own
            back_ax += there * own
        return back_rad, back_ax

    block(src)

    lane = iota((CYC, CYC), 1)
    sub = iota((CYC, CYC), 0)
    tile_rows = jnp.broadcast_to(tile_of, (CYC, CYC))
    same = (jnp.transpose(tile_rows) == tile_rows) & ((sub >> 1) < (lane >> 1))
    rank = jnp.sum(same.astype(F32), axis=0, keepdims=True)
    slot = rank.astype(jnp.int32) + (iota((1, CYC), 1) & 1)
    route = (sub == jnp.broadcast_to(tile_row, (CYC, CYC))).astype(F32)

    pl.semaphore_wait(barrier, 65)

    def send_source(kr, kc):
        pltpu.make_async_remote_copy(
            src_ref=src,
            dst_ref=ag.at[kr, kc],
            send_sem=ag_ssem,
            recv_sem=ag_rsem.at[kr, kc],
            device_id=before(kr, kc),
            device_id_type=MESH,
        ).start()

    each_shift(send_source)

    def arrive(kr, kc):
        pltpu.make_async_copy(src, ag.at[kr, kc], ag_rsem.at[kr, kc]).wait()

    def meet(kr, kc):
        back_rad, back_ax = block(ag.at[kr, kc])
        ret_send[kr, kc, 0:1] = jnp.sum(back_rad, axis=0, keepdims=True)
        ret_send[kr, kc, 1:2] = jnp.sum(back_ax, axis=0, keepdims=True)

    def send_back(kr, kc):
        pltpu.make_async_remote_copy(
            src_ref=ret_send.at[kr, kc],
            dst_ref=ret_recv.at[kr, kc],
            send_sem=ret_sem.at[0],
            recv_sem=ret_sem.at[1],
            device_id=at(kr, kc),
            device_id_type=MESH,
        ).start()

    def arrive_meet(kr, kc):
        arrive(kr, kc)
        meet(kr, kc)

    def full_meet(kr, kc):
        arrive_meet(kr, kc)
        send_back(kr, kc)

    for segment in segments:
        over(segment, full_meet if segment[-1] else arrive_meet)

    def wait_bytes(ref, count, sem):
        view = ref.at[pl.ds(0, count)]
        pltpu.make_async_copy(view, view, sem).wait()

    own_rad = jnp.sum(jnp.transpose(acc_rad[...]), axis=0, keepdims=True)
    own_ax = jnp.sum(jnp.transpose(acc_ax[...]), axis=0, keepdims=True)

    flat = ret_recv.reshape(5 * N_COL, 2, CYC)
    wait_bytes(flat, 62, ret_sem.at[1])
    got = jnp.sum(ret_recv[1:4], axis=(0, 1))
    got += jnp.sum(ret_recv[0, 1:8], axis=0) + jnp.sum(ret_recv[4, 1:8], axis=0)
    disp_r = (own_rad - got[0:1]) / pos_r
    disp_z = own_ax + got[1:2]
    disp_ref[0:1] = disp_r
    disp_ref[1:2] = disp_z

    moved_r = jnp.clip(offs[0:1] + disp_r, -1.0, 2.0)
    moved_z = jnp.clip(offs[1:2] + disp_z, -1.0, 2.0)
    local_r = (cell_r - part * CR).astype(F32)
    local_z = (cell_z - slab * CZ).astype(F32)
    blank = jnp.zeros((3, CYC), F32)
    values = jnp.concatenate([local_r, moved_r, local_z, moved_z, strength, blank], axis=0)
    payload = jnp.concatenate([jnp.where(slot == s, values, 0.0) for s in range(4)], axis=0)
    payload = jnp.concatenate([payload, jnp.zeros((96, CYC), F32)], axis=0)
    out1[:, 0, :] = dot(route, payload, ((1,), (1,)), HIGH)

    me = row * N_COL + col

    def to_all(out, into, sem):
        def outer(i, carry):
            kr = lax.rem(3 * i + 3, N_ROW)
            dr = lax.rem(row + kr, N_ROW)

            def send(dc):
                pltpu.make_async_remote_copy(
                    src_ref=out.at[dr * N_COL + dc],
                    dst_ref=into.at[me],
                    send_sem=sem.at[0],
                    recv_sem=sem.at[1],
                    device_id=(dr, dc),
                    device_id_type=MESH,
                ).start()

            for kc in range(1, N_COL):
                send(lax.rem(col + kc, N_COL))

            @pl.when(kr > 0)
            def _():
                send(col)

            return carry

        lax.fori_loop(0, N_ROW, outer, 0)
        into[me] = out[me]
        wait_bytes(into, DEVICES - 1, sem.at[1])

    to_all(out1, in1, a1_sem)

    across = jnp.transpose(in1[:, 0, :])

    def spread(value):
        return jnp.concatenate([across[8 * s + value : 8 * s + value + 1] for s in range(4)], axis=1)

    cell_r4, moved_r4, cell_z4, moved_z4, power = (spread(v) for v in range(5))
    wrapped = iota((16, SLOTS), 0) & 7
    wrapped = wrapped - jnp.where(wrapped < 4, 0, 8)
    first = iota((16, SLOTS), 0) < 8
    edge_z = tent(((wrapped + jnp.where(first, CZ, 0)).astype(F32) - cell_z4) - moved_z4)
    edge_r = tent(((wrapped + jnp.where(first, CR, 0)).astype(F32) - cell_r4) - moved_r4) * power
    edge_z, edge_r = halves(edge_z), halves(edge_r)
    corners = dot3(edge_z, edge_r, ((1,), (1,)))
    corners = jnp.concatenate([corners, jnp.zeros((16, 112), F32)], axis=1)
    co_send[0] = corners[0:8]
    co_send[1] = corners[8:16]

    next_r, prev_r = lax.rem(row + 1, N_ROW), lax.rem(row + N_ROW - 1, N_ROW)
    next_c, prev_c = lax.rem(col + 1, N_COL), lax.rem(col + N_COL - 1, N_COL)
    copies = []

    def give(source, target, device):
        i = len(copies)
        copy = pltpu.make_async_remote_copy(
            src_ref=source,
            dst_ref=target,
            send_sem=halo_ssem.at[i],
            recv_sem=halo_rsem.at[i],
            device_id=device,
            device_id_type=MESH,
        )
        copy.start()
        copies.append(copy)

    give(co_send.at[0], co_recv.at[0], (next_r, next_c))
    give(co_send.at[0], co_recv.at[1], (next_r, prev_c))
    give(co_send.at[1], co_recv.at[2], (prev_r, next_c))
    give(co_send.at[1], co_recv.at[3], (prev_r, prev_c))

    step = iota((EXT_R, SLOTS), 0)
    cell_of_row = jnp.where(step < 260, step, step - EXT_R).astype(F32)
    radial = tent((cell_of_row - cell_r4) - moved_r4)
    loaded_h, loaded_l = halves(radial * power)
    strips = dot3(edge_z, (loaded_h, loaded_l), ((1,), (1,)))
    strips = jnp.concatenate([strips, jnp.zeros((16, 384 - EXT_R), F32)], axis=1)
    ew_send[0] = strips[0:8]
    ew_send[1] = strips[8:16]
    give(ew_send.at[0], ew_recv.at[0], (next_r, col))
    give(ew_send.at[1], ew_recv.at[1], (prev_r, col))

    def axial(i, carry):
        start = jnp.where(i < 34, i * 32, i * 32 - EXT_Z)
        cell = (iota((32, SLOTS), 0) + start).astype(F32)
        high, low = halves(tent((cell - cell_z4) - moved_z4))
        rows = pl.ds(pl.multiple_of(i * 32, 32), 32)
        zh[rows] = high
        zl[rows] = low
        return carry

    lax.fori_loop(0, EXT_Z // 32, axial, 0, unroll=1)
    weights = (zh[...], zl[...])
    loaded = tuple(jnp.concatenate(pair, axis=0) for pair in zip((loaded_h, loaded_l), edge_r))
    both = dot3(loaded, weights, ((1,), (1,)))
    ns_send[0] = both[EXT_R : EXT_R + 8]
    ns_send[1] = both[EXT_R + 8 :]
    give(ns_send.at[0], ns_recv.at[0], (row, next_c))
    give(ns_send.at[1], ns_recv.at[1], (row, prev_c))
    dep[...] = both[:EXT_R]

    for copy in copies:
        copy.wait_recv()

    has_next_r, has_prev_r = row < N_ROW - 1, row > 0
    has_next_c, has_prev_c = col < N_COL - 1, col > 0
    strip_lane = iota((8, CYC), 1)

    def side(i, present):
        wide = jnp.where(present, ew_recv[i], 0.0)
        first, second, third = wide[:, 0:128], wide[:, 128:256], wide[:, 256:384]
        third = jnp.where(strip_lane < 8, third, 0.0)
        low = jnp.where(has_prev_c & present, co_recv[2 * i], 0.0)
        high = jnp.where(has_next_c & present, co_recv[2 * i + 1], 0.0)
        first += jnp.where(strip_lane < 4, low, 0.0)
        third += jnp.where((strip_lane >= 4) & (strip_lane < 8), low, 0.0)
        third += jnp.where(strip_lane < 4, pltpu.roll(high, 120, axis=1), 0.0)
        second += jnp.where(strip_lane >= 124, pltpu.roll(high, 112, axis=1), 0.0)
        wide = jnp.concatenate([first, second, third], axis=1)
        upper = iota((8, 384), 0) < 4
        wide = jnp.concatenate(
            [jnp.where(upper, wide, 0.0), jnp.zeros((112, 384), F32), jnp.where(upper, 0.0, wide)],
            axis=0,
        )
        return jnp.transpose(wide)[0:EXT_R]

    left = side(0, has_prev_r)
    right = side(1, has_next_r)
    front = iota((EXT_R, 128), 1) < 64
    dep[:, 0:128] += jnp.where(front, left, 0.0)
    dep[:, 896:1024] += jnp.where(front, 0.0, right)
    dep[:, 1024:1152] += jnp.where(front, right, left)
    upper = iota((8, EXT_Z), 0) < 4
    above = jnp.where(has_prev_c, ns_recv[0], 0.0)
    below = jnp.where(has_next_c, ns_recv[1], 0.0)
    dep[0:8] += jnp.where(upper, above, 0.0)
    dep[248:256] += jnp.where(upper, 0.0, below)
    dep[256:264] += jnp.where(upper, below, above)

    base = col * CR
    for i in range(EXT_R // 8):
        here = dep[8 * i : 8 * i + 8]
        prev = dep[8 * i - 8 : 8 * i] if i else dep[EXT_R - 8 : EXT_R]
        nxt = dep[8 * i + 8 : 8 * i + 16] if i < EXT_R // 8 - 1 else dep[0:8]
        inward = jnp.concatenate([prev[7:8], here[0:7]], axis=0)
        outward = jnp.concatenate([here[1:8], nxt[0:1]], axis=0)
        forward = pltpu.roll(here, EXT_Z - 1, axis=1)
        backward = pltpu.roll(here, 1, axis=1)
        number = iota((8, 128), 0) + 8 * i
        number = jnp.where(number < 260, number, number - EXT_R) + base
        radius = jnp.maximum(number, 1).astype(F32)
        half = jnp.concatenate([0.5 / radius] * 9, axis=1)
        square = jnp.concatenate([1.0 / (radius * radius)] * 9, axis=1)
        laplace = (
            (outward + inward)
            + (forward + backward)
            - 4.0 * here
            + (outward - inward) * half
            - here * square
        )
        new = here + VISCOSITY * laplace
        fld[8 * i : 8 * i + 8] = new
        if i < CR // 8:
            diff_ref[8 * i : 8 * i + 8] = new[:, 0:CZ]

    read = dot3(halves(fld[...]), (zh[...], zl[...]), ((1,), (0,)))
    found = jnp.sum(read * radial, axis=0, keepdims=True)
    found = jnp.concatenate(
        [found[:, CYC * s : CYC * s + CYC] for s in range(4)] + [jnp.zeros((124, CYC), F32)], axis=0
    )
    out2[:, 0, :] = jnp.transpose(found)
    to_all(out2, in2, a2_sem)
    table = jnp.transpose(in2[:, 0, :])[0:8]
    mine = dot(table, route, ((1,), (0,)), HIGH)
    renew_ref[...] = jnp.sum(
        jnp.where(iota((8, CYC), 0) == slot, mine, 0.0), axis=0, keepdims=True
    )

    sent = ag.reshape(5 * N_COL, 4, CYC)
    wait_bytes(sent, 65, ag_ssem)
    wait_bytes(flat, 62, ret_sem.at[0])
    wait_bytes(out1, DEVICES - 1, a1_sem.at[0])
    wait_bytes(out2, DEVICES - 1, a2_sem.at[0])
    for copy in copies:
        copy.wait_send()


def write_out(disp_ref, diff_ref, renew_ref, disp_out, diff_out, renew_out, sem):
    pairs = [(disp_ref, disp_out), (renew_ref, renew_out)]
    for i in range(8):
        rows = pl.ds(i * CR // 8, CR // 8)
        pairs.append((diff_ref.at[rows], diff_out.at[rows]))
    copies = [
        pltpu.make_async_copy(source, target, sem.at[i])
        for i, (source, target) in enumerate(pairs)
    ]
    for copy in copies:
        copy.start()
    for copy in copies:
        copy.wait()


def on_device(cycle_cells, cycle_offsets, cycle_strength, block_tile):
    vmem = pl.BlockSpec(memory_space=pltpu.VMEM)
    hbm = pl.BlockSpec(memory_space=pl.ANY)
    dma = pltpu.SemaphoreType.DMA
    shapes = [
        jax.ShapeDtypeStruct((2, CYC), F32),
        jax.ShapeDtypeStruct((CR, CZ), F32),
        jax.ShapeDtypeStruct((1, CYC), F32),
    ]
    results = pl.pallas_call(
        kernel,
        out_shape=shapes,
        in_specs=[vmem] * 4,
        out_specs=[vmem] * 3,
        scratch_shapes=[
            pltpu.VMEM((4, CYC), F32),
            pltpu.VMEM((5, N_COL, 4, CYC), F32),
            pltpu.VMEM((5, N_COL, 2, CYC), F32),
            pltpu.VMEM((5, N_COL, 2, CYC), F32),
            pltpu.VMEM((CYC, CYC), F32),
            pltpu.VMEM((CYC, CYC), F32),
            pltpu.VMEM((CYC, CYC), F32),
            pltpu.VMEM((CYC, CYC), F32),
            pltpu.VMEM((CYC, CYC), F32),
            pltpu.VMEM((CYC, CYC), F32),
            pltpu.VMEM((DEVICES, 1, CYC), F32),
            pltpu.VMEM((DEVICES, 1, CYC), F32),
            pltpu.VMEM((DEVICES, 1, CYC), F32),
            pltpu.VMEM((DEVICES, 1, CYC), F32),
            pltpu.VMEM((EXT_Z, SLOTS), BF16),
            pltpu.VMEM((EXT_Z, SLOTS), BF16),
            pltpu.VMEM((2, 8, EXT_Z), F32),
            pltpu.VMEM((2, 8, EXT_Z), F32),
            pltpu.VMEM((2, 8, 384), F32),
            pltpu.VMEM((2, 8, 384), F32),
            pltpu.VMEM((2, 8, 128), F32),
            pltpu.VMEM((4, 8, 128), F32),
            pltpu.VMEM((EXT_R, EXT_Z), F32),
            pltpu.VMEM((EXT_R, EXT_Z), F32),
            dma,
            dma((5, N_COL)),
            dma((2,)),
            dma((2,)),
            dma((8,)),
            dma((8,)),
            dma((2,)),
        ],
        compiler_params=pltpu.CompilerParams(
            collective_id=0, has_side_effects=True, vmem_limit_bytes=40 * 2**20
        ),
    )(cycle_cells, cycle_offsets, cycle_strength.reshape(1, CYC), block_tile.reshape(1, -1))
    displacement, diffused, renewed = pl.pallas_call(
        write_out,
        out_shape=shapes,
        in_specs=[vmem] * 3,
        out_specs=[hbm] * 3,
        scratch_shapes=[dma((10,))],
        compiler_params=pltpu.CompilerParams(vmem_limit_bytes=2**20),
    )(*results)
    return displacement, diffused, renewed.reshape(CYC)


def solution(mesh):
    in_specs = (
        P(None, ("row", "col")),
        P(None, ("row", "col")),
        P(("row", "col")),
        P(("row", "col")),
    )
    out_specs = (P(None, ("row", "col")), P("col", "row"), P(("row", "col")))
    return jax.shard_map(
        on_device, mesh=mesh, in_specs=in_specs, out_specs=out_specs, check_vma=False
    )
```

```python
import jax
import jax.numpy as jnp
from jax import lax
from jax.experimental import pallas as pl
from jax.experimental.pallas import tpu as pltpu
from jax.sharding import PartitionSpec as P

MESH = pl.DeviceIdType.MESH
F32 = jnp.float32
BF16 = jnp.bfloat16
HIGH = lax.Precision.HIGHEST

N_ROW = 8
N_COL = 16
DEVICES = N_ROW * N_COL
CYC = 128
CR = 256
CZ = 1024
EXT_R = 264
EXT_Z = 1152
SLOTS = 512
VISCOSITY = 0.2
CORE_SQUARE = 4.0
STEP_LENGTH = 4.0
CHUNK = 128


def iota(shape, dim):
    return lax.broadcasted_iota(jnp.int32, shape, dim)


def dot(a, b, contract, precision=None):
    return lax.dot_general(
        a, b, (contract, ((), ())), precision=precision, preferred_element_type=F32
    )


def halves(x):
    high = x.astype(BF16)
    return high, (x - high.astype(F32)).astype(BF16)


def dot3(a, b, contract):
    (ah, al), (bh, bl) = a, b
    ka, kb = contract[0][0], contract[1][0]
    left = jnp.concatenate([ah, ah, al], axis=ka)
    return dot(left, jnp.concatenate([bh, bl, bh], axis=kb), contract)


def tent(x):
    return jnp.maximum(1.0 - jnp.abs(x), 0.0)


def pair_terms(r, rr, z, a, a2, aa, src_z):
    d = z - src_z
    gap = a - r
    s = d * d + CORE_SQUARE
    near = s + gap * gap
    w = a2 * r
    u = near + w
    pq = (u + w) * near
    g = pq * lax.rsqrt(pq)
    b = g * lax.rsqrt(g)
    x = (u + g) * 0.5
    a = x * lax.rsqrt(x)
    t = []
    for _ in range(4):
        product = a * b
        t.append(product)
        a = (a + b) * 0.5
        b = product * lax.rsqrt(product)
    twice = a + b
    h = t[3]
    for n in (2, 1, 0):
        h = (h + h) + t[n]
    e = (8.0 * twice) * twice - ((h + h) + g)
    inverse = 1.0 / twice
    y = (e * inverse) * (1.0 / pq)
    radial = (u * y - inverse) * d
    even = inverse - y * s
    odd = y * (aa - rr)
    return radial, even + odd, even - odd


def kernel(
    cells_ref, offs_ref, stren_ref, btile_ref,
    disp_ref, diff_ref, renew_ref,
    src, ag, ret_send, ret_recv, tr, tz, tg, trr, acc_rad, acc_ax,
    out1, in1, out2, in2, zh, zl, ns_send, ns_recv, ew_send, ew_recv, co_send, co_recv, dep, fld,
    ag_ssem, ag_rsem, ret_sem, a1_sem, halo_ssem, halo_rsem, a2_sem,
):
    row = lax.axis_index("row")
    col = lax.axis_index("col")

    def at(kr, kc):
        return lax.rem(row + kr, N_ROW), lax.rem(col + kc, N_COL)

    def before(kr, kc):
        return lax.rem(row + (N_ROW - kr), N_ROW), lax.rem(col + (N_COL - kc), N_COL)

    segments = [
        (4, lambda i: 0, lambda i: 4 + i, True),
        (8, lambda i: 2, lambda i: i, True),
        (7, lambda i: 4, lambda i: 1 + i, True),
        (32, lambda i: 3 - 2 * (i // N_COL), lambda i: lax.rem(i, N_COL), True),
        (8, lambda i: 2, lambda i: 8 + i, True),
        (3, lambda i: 0, lambda i: 3 - i, True),
        (3, lambda i: 4 * ((i + 1) // 2), lambda i: 8 * (1 - i // 2), False),
    ]

    def over(segment, body):
        count, kr, kc, _ = segment

        def one(i, carry):
            body(kr(i), kc(i))
            return carry

        lax.fori_loop(0, count, one, 0)

    def each_shift(body):
        for segment in segments:
            over(segment, body)

    barrier = pltpu.get_barrier_semaphore()

    def greet(kr, kc):
        pl.semaphore_signal(barrier, inc=1, device_id=at(kr, kc), device_id_type=MESH)

    each_shift(greet)

    widen = (iota((64, CYC), 1) // 2 == iota((64, CYC), 0)).astype(F32)
    tile_of = dot(
        jnp.broadcast_to(btile_ref[...].astype(F32), (8, 64)), widen, ((1,), (0,)), HIGH
    )[0:1]
    tile_row = tile_of.astype(jnp.int32)
    part = tile_row & (N_COL - 1)
    slab = tile_row >> 4
    cell_r = jnp.clip(part * CR + cells_ref[0:1], 16, CR * N_COL - 3)
    cell_z = jnp.clip(slab * CZ + cells_ref[1:2], 2, CZ * N_ROW - 3)
    offs = offs_ref[...]
    pos_r = cell_r.astype(F32) + offs[0:1]
    pos_z = cell_z.astype(F32) + offs[1:2]
    strength = stren_ref[...]
    src[0:1] = pos_r
    src[1:2] = pos_z
    src[2:3] = (STEP_LENGTH * 0.5) * strength
    src[3:4] = jnp.zeros((1, CYC), F32)

    def column(v):
        return jnp.transpose(jnp.broadcast_to(v, (CYC, CYC)))

    tr[...] = column(pos_r)
    tz[...] = column(pos_z)
    tg[...] = column((STEP_LENGTH * 0.5) * strength)
    trr[...] = tr[...] * tr[...]
    acc_rad[...] = jnp.zeros((CYC, CYC), F32)
    acc_ax[...] = jnp.zeros((CYC, CYC), F32)

    def block(ref):
        a = ref[0:1, :]
        src_z = ref[1:2, :]
        src_g = ref[2:3, :]
        a, a2, aa, src_z, src_g = (
            jnp.broadcast_to(v, (CHUNK, CYC)) for v in (a, a + a, a * a, src_z, src_g)
        )
        back_rad = jnp.zeros((CHUNK, CYC), F32)
        back_ax = jnp.zeros((CHUNK, CYC), F32)
        for i in range(CYC // CHUNK):
            rows = pl.ds(i * CHUNK, CHUNK)
            radial, here, there = pair_terms(tr[rows], trr[rows], tz[rows], a, a2, aa, src_z)
            acc_rad[rows] += radial * src_g
            acc_ax[rows] += here * src_g
            own = tg[rows]
            back_rad += radial * own
            back_ax += there * own
        return back_rad, back_ax

    block(src)

    lane = iota((CYC, CYC), 1)
    sub = iota((CYC, CYC), 0)
    tile_rows = jnp.broadcast_to(tile_of, (CYC, CYC))
    same = (jnp.transpose(tile_rows) == tile_rows) & ((sub >> 1) < (lane >> 1))
    rank = jnp.sum(same.astype(F32), axis=0, keepdims=True)
    slot = rank.astype(jnp.int32) + (iota((1, CYC), 1) & 1)
    route = (sub == jnp.broadcast_to(tile_row, (CYC, CYC))).astype(F32)

    pl.semaphore_wait(barrier, 65)

    def send_source(kr, kc):
        pltpu.make_async_remote_copy(
            src_ref=src,
            dst_ref=ag.at[kr, kc],
            send_sem=ag_ssem,
            recv_sem=ag_rsem.at[kr, kc],
            device_id=before(kr, kc),
            device_id_type=MESH,
        ).start()

    each_shift(send_source)

    def arrive(kr, kc):
        pltpu.make_async_copy(src, ag.at[kr, kc], ag_rsem.at[kr, kc]).wait()

    def meet(kr, kc):
        back_rad, back_ax = block(ag.at[kr, kc])
        ret_send[kr, kc, 0:1] = jnp.sum(back_rad, axis=0, keepdims=True)
        ret_send[kr, kc, 1:2] = jnp.sum(back_ax, axis=0, keepdims=True)

    def send_back(kr, kc):
        pltpu.make_async_remote_copy(
            src_ref=ret_send.at[kr, kc],
            dst_ref=ret_recv.at[kr, kc],
            send_sem=ret_sem.at[0],
            recv_sem=ret_sem.at[1],
            device_id=at(kr, kc),
            device_id_type=MESH,
        ).start()

    def arrive_meet(kr, kc):
        arrive(kr, kc)
        meet(kr, kc)

    def full_meet(kr, kc):
        arrive_meet(kr, kc)
        send_back(kr, kc)

    for segment in segments:
        over(segment, full_meet if segment[-1] else arrive_meet)

    def wait_bytes(ref, count, sem):
        view = ref.at[pl.ds(0, count)]
        pltpu.make_async_copy(view, view, sem).wait()

    own_rad = jnp.sum(jnp.transpose(acc_rad[...]), axis=0, keepdims=True)
    own_ax = jnp.sum(jnp.transpose(acc_ax[...]), axis=0, keepdims=True)

    flat = ret_recv.reshape(5 * N_COL, 2, CYC)
    wait_bytes(flat, 62, ret_sem.at[1])
    got = jnp.sum(ret_recv[1:4], axis=(0, 1))
    got += jnp.sum(ret_recv[0, 1:8], axis=0) + jnp.sum(ret_recv[4, 1:8], axis=0)
    disp_r = (own_rad - got[0:1]) / pos_r
    disp_z = own_ax + got[1:2]
    disp_ref[0:1] = disp_r
    disp_ref[1:2] = disp_z

    moved_r = jnp.clip(offs[0:1] + disp_r, -1.0, 2.0)
    moved_z = jnp.clip(offs[1:2] + disp_z, -1.0, 2.0)
    local_r = (cell_r - part * CR).astype(F32)
    local_z = (cell_z - slab * CZ).astype(F32)
    blank = jnp.zeros((3, CYC), F32)
    values = jnp.concatenate([local_r, moved_r, local_z, moved_z, strength, blank], axis=0)
    payload = jnp.concatenate([jnp.where(slot == s, values, 0.0) for s in range(4)], axis=0)
    payload = jnp.concatenate([payload, jnp.zeros((96, CYC), F32)], axis=0)
    out1[:, 0, :] = dot(route, payload, ((1,), (1,)), HIGH)

    me = row * N_COL + col

    def to_all(out, into, sem):
        def outer(i, carry):
            kr = lax.rem(3 * i + 3, N_ROW)
            dr = lax.rem(row + kr, N_ROW)

            def send(dc):
                pltpu.make_async_remote_copy(
                    src_ref=out.at[dr * N_COL + dc],
                    dst_ref=into.at[me],
                    send_sem=sem.at[0],
                    recv_sem=sem.at[1],
                    device_id=(dr, dc),
                    device_id_type=MESH,
                ).start()

            for kc in range(1, N_COL):
                send(lax.rem(col + kc, N_COL))

            @pl.when(kr > 0)
            def _():
                send(col)

            return carry

        lax.fori_loop(0, N_ROW, outer, 0)
        into[me] = out[me]
        wait_bytes(into, DEVICES - 1, sem.at[1])

    to_all(out1, in1, a1_sem)

    across = jnp.transpose(in1[:, 0, :])

    def spread(value):
        return jnp.concatenate([across[8 * s + value : 8 * s + value + 1] for s in range(4)], axis=1)

    cell_r4, moved_r4, cell_z4, moved_z4, power = (spread(v) for v in range(5))
    wrapped = iota((16, SLOTS), 0) & 7
    wrapped = wrapped - jnp.where(wrapped < 4, 0, 8)
    first = iota((16, SLOTS), 0) < 8
    edge_z = tent(((wrapped + jnp.where(first, CZ, 0)).astype(F32) - cell_z4) - moved_z4)
    edge_r = tent(((wrapped + jnp.where(first, CR, 0)).astype(F32) - cell_r4) - moved_r4) * power
    edge_z, edge_r = halves(edge_z), halves(edge_r)
    corners = dot3(edge_z, edge_r, ((1,), (1,)))
    corners = jnp.concatenate([corners, jnp.zeros((16, 112), F32)], axis=1)
    co_send[0] = corners[0:8]
    co_send[1] = corners[8:16]

    next_r, prev_r = lax.rem(row + 1, N_ROW), lax.rem(row + N_ROW - 1, N_ROW)
    next_c, prev_c = lax.rem(col + 1, N_COL), lax.rem(col + N_COL - 1, N_COL)
    copies = []

    def give(source, target, device):
        i = len(copies)
        copy = pltpu.make_async_remote_copy(
            src_ref=source,
            dst_ref=target,
            send_sem=halo_ssem.at[i],
            recv_sem=halo_rsem.at[i],
            device_id=device,
            device_id_type=MESH,
        )
        copy.start()
        copies.append(copy)

    give(co_send.at[0], co_recv.at[0], (next_r, next_c))
    give(co_send.at[0], co_recv.at[1], (next_r, prev_c))
    give(co_send.at[1], co_recv.at[2], (prev_r, next_c))
    give(co_send.at[1], co_recv.at[3], (prev_r, prev_c))

    step = iota((EXT_R, SLOTS), 0)
    cell_of_row = jnp.where(step < 260, step, step - EXT_R).astype(F32)
    radial = tent((cell_of_row - cell_r4) - moved_r4)
    loaded_h, loaded_l = halves(radial * power)
    strips = dot3(edge_z, (loaded_h, loaded_l), ((1,), (1,)))
    strips = jnp.concatenate([strips, jnp.zeros((16, 384 - EXT_R), F32)], axis=1)
    ew_send[0] = strips[0:8]
    ew_send[1] = strips[8:16]
    give(ew_send.at[0], ew_recv.at[0], (next_r, col))
    give(ew_send.at[1], ew_recv.at[1], (prev_r, col))

    def axial(i, carry):
        start = jnp.where(i < 34, i * 32, i * 32 - EXT_Z)
        cell = (iota((32, SLOTS), 0) + start).astype(F32)
        high, low = halves(tent((cell - cell_z4) - moved_z4))
        rows = pl.ds(pl.multiple_of(i * 32, 32), 32)
        zh[rows] = high
        zl[rows] = low
        return carry

    lax.fori_loop(0, EXT_Z // 32, axial, 0, unroll=1)
    weights = (zh[...], zl[...])
    loaded = tuple(jnp.concatenate(pair, axis=0) for pair in zip((loaded_h, loaded_l), edge_r))
    both = dot3(loaded, weights, ((1,), (1,)))
    ns_send[0] = both[EXT_R : EXT_R + 8]
    ns_send[1] = both[EXT_R + 8 :]
    give(ns_send.at[0], ns_recv.at[0], (row, next_c))
    give(ns_send.at[1], ns_recv.at[1], (row, prev_c))
    dep[...] = both[:EXT_R]

    for copy in copies:
        copy.wait_recv()

    has_next_r, has_prev_r = row < N_ROW - 1, row > 0
    has_next_c, has_prev_c = col < N_COL - 1, col > 0
    strip_lane = iota((8, CYC), 1)

    def side(i, present):
        wide = jnp.where(present, ew_recv[i], 0.0)
        first, second, third = wide[:, 0:128], wide[:, 128:256], wide[:, 256:384]
        third = jnp.where(strip_lane < 8, third, 0.0)
        low = jnp.where(has_prev_c & present, co_recv[2 * i], 0.0)
        high = jnp.where(has_next_c & present, co_recv[2 * i + 1], 0.0)
        first += jnp.where(strip_lane < 4, low, 0.0)
        third += jnp.where((strip_lane >= 4) & (strip_lane < 8), low, 0.0)
        third += jnp.where(strip_lane < 4, pltpu.roll(high, 120, axis=1), 0.0)
        second += jnp.where(strip_lane >= 124, pltpu.roll(high, 112, axis=1), 0.0)
        wide = jnp.concatenate([first, second, third], axis=1)
        upper = iota((8, 384), 0) < 4
        wide = jnp.concatenate(
            [jnp.where(upper, wide, 0.0), jnp.zeros((112, 384), F32), jnp.where(upper, 0.0, wide)],
            axis=0,
        )
        return jnp.transpose(wide)[0:EXT_R]

    left = side(0, has_prev_r)
    right = side(1, has_next_r)
    front = iota((EXT_R, 128), 1) < 64
    dep[:, 0:128] += jnp.where(front, left, 0.0)
    dep[:, 896:1024] += jnp.where(front, 0.0, right)
    dep[:, 1024:1152] += jnp.where(front, right, left)
    upper = iota((8, EXT_Z), 0) < 4
    above = jnp.where(has_prev_c, ns_recv[0], 0.0)
    below = jnp.where(has_next_c, ns_recv[1], 0.0)
    dep[0:8] += jnp.where(upper, above, 0.0)
    dep[248:256] += jnp.where(upper, 0.0, below)
    dep[256:264] += jnp.where(upper, below, above)

    base = col * CR
    for i in range(EXT_R // 8):
        here = dep[8 * i : 8 * i + 8]
        prev = dep[8 * i - 8 : 8 * i] if i else dep[EXT_R - 8 : EXT_R]
        nxt = dep[8 * i + 8 : 8 * i + 16] if i < EXT_R // 8 - 1 else dep[0:8]
        inward = jnp.concatenate([prev[7:8], here[0:7]], axis=0)
        outward = jnp.concatenate([here[1:8], nxt[0:1]], axis=0)
        forward = pltpu.roll(here, EXT_Z - 1, axis=1)
        backward = pltpu.roll(here, 1, axis=1)
        number = iota((8, 128), 0) + 8 * i
        number = jnp.where(number < 260, number, number - EXT_R) + base
        radius = jnp.maximum(number, 1).astype(F32)
        half = jnp.concatenate([0.5 / radius] * 9, axis=1)
        square = jnp.concatenate([1.0 / (radius * radius)] * 9, axis=1)
        laplace = (
            (outward + inward)
            + (forward + backward)
            - 4.0 * here
            + (outward - inward) * half
            - here * square
        )
        new = here + VISCOSITY * laplace
        fld[8 * i : 8 * i + 8] = new
        if i < CR // 8:
            diff_ref[8 * i : 8 * i + 8] = new[:, 0:CZ]

    read = dot3(halves(fld[...]), (zh[...], zl[...]), ((1,), (0,)))
    found = jnp.sum(read * radial, axis=0, keepdims=True)
    found = jnp.concatenate(
        [found[:, CYC * s : CYC * s + CYC] for s in range(4)] + [jnp.zeros((124, CYC), F32)], axis=0
    )
    out2[:, 0, :] = jnp.transpose(found)
    to_all(out2, in2, a2_sem)
    table = jnp.transpose(in2[:, 0, :])[0:8]
    mine = dot(table, route, ((1,), (0,)), HIGH)
    renew_ref[...] = jnp.sum(
        jnp.where(iota((8, CYC), 0) == slot, mine, 0.0), axis=0, keepdims=True
    )

    sent = ag.reshape(5 * N_COL, 4, CYC)
    wait_bytes(sent, 65, ag_ssem)
    wait_bytes(flat, 62, ret_sem.at[0])
    wait_bytes(out1, DEVICES - 1, a1_sem.at[0])
    wait_bytes(out2, DEVICES - 1, a2_sem.at[0])
    for copy in copies:
        copy.wait_send()


def write_out(disp_ref, diff_ref, renew_ref, disp_out, diff_out, renew_out, sem):
    pairs = [(disp_ref, disp_out), (renew_ref, renew_out)]
    for i in range(8):
        rows = pl.ds(i * CR // 8, CR // 8)
        pairs.append((diff_ref.at[rows], diff_out.at[rows]))
    copies = [
        pltpu.make_async_copy(source, target, sem.at[i])
        for i, (source, target) in enumerate(pairs)
    ]
    for copy in copies:
        copy.start()
    for copy in copies:
        copy.wait()


def on_device(cycle_cells, cycle_offsets, cycle_strength, block_tile):
    vmem = pl.BlockSpec(memory_space=pltpu.VMEM)
    hbm = pl.BlockSpec(memory_space=pl.ANY)
    dma = pltpu.SemaphoreType.DMA
    shapes = [
        jax.ShapeDtypeStruct((2, CYC), F32),
        jax.ShapeDtypeStruct((CR, CZ), F32),
        jax.ShapeDtypeStruct((1, CYC), F32),
    ]
    results = pl.pallas_call(
        kernel,
        out_shape=shapes,
        in_specs=[vmem] * 4,
        out_specs=[vmem] * 3,
        scratch_shapes=[
            pltpu.VMEM((4, CYC), F32),
            pltpu.VMEM((5, N_COL, 4, CYC), F32),
            pltpu.VMEM((5, N_COL, 2, CYC), F32),
            pltpu.VMEM((5, N_COL, 2, CYC), F32),
            pltpu.VMEM((CYC, CYC), F32),
            pltpu.VMEM((CYC, CYC), F32),
            pltpu.VMEM((CYC, CYC), F32),
            pltpu.VMEM((CYC, CYC), F32),
            pltpu.VMEM((CYC, CYC), F32),
            pltpu.VMEM((CYC, CYC), F32),
            pltpu.VMEM((DEVICES, 1, CYC), F32),
            pltpu.VMEM((DEVICES, 1, CYC), F32),
            pltpu.VMEM((DEVICES, 1, CYC), F32),
            pltpu.VMEM((DEVICES, 1, CYC), F32),
            pltpu.VMEM((EXT_Z, SLOTS), BF16),
            pltpu.VMEM((EXT_Z, SLOTS), BF16),
            pltpu.VMEM((2, 8, EXT_Z), F32),
            pltpu.VMEM((2, 8, EXT_Z), F32),
            pltpu.VMEM((2, 8, 384), F32),
            pltpu.VMEM((2, 8, 384), F32),
            pltpu.VMEM((2, 8, 128), F32),
            pltpu.VMEM((4, 8, 128), F32),
            pltpu.VMEM((EXT_R, EXT_Z), F32),
            pltpu.VMEM((EXT_R, EXT_Z), F32),
            dma,
            dma((5, N_COL)),
            dma((2,)),
            dma((2,)),
            dma((8,)),
            dma((8,)),
            dma((2,)),
        ],
        compiler_params=pltpu.CompilerParams(
            collective_id=0, has_side_effects=True, vmem_limit_bytes=40 * 2**20
        ),
    )(cycle_cells, cycle_offsets, cycle_strength.reshape(1, CYC), block_tile.reshape(1, -1))
    displacement, diffused, renewed = pl.pallas_call(
        write_out,
        out_shape=shapes,
        in_specs=[vmem] * 3,
        out_specs=[hbm] * 3,
        scratch_shapes=[dma((10,))],
        compiler_params=pltpu.CompilerParams(vmem_limit_bytes=2**20),
    )(*results)
    return displacement, diffused, renewed.reshape(CYC)


def solution(mesh):
    in_specs = (
        P(None, ("row", "col")),
        P(None, ("row", "col")),
        P(("row", "col")),
        P(("row", "col")),
    )
    out_specs = (P(None, ("row", "col")), P("col", "row"), P(("row", "col")))
    return jax.shard_map(
        on_device, mesh=mesh, in_specs=in_specs, out_specs=out_specs, check_vma=False
    )
```

```python
import jax
import jax.numpy as jnp
from jax import lax
from jax.experimental import pallas as pl
from jax.experimental.pallas import tpu as pltpu
from jax.sharding import PartitionSpec as P

MESH = pl.DeviceIdType.MESH
F32 = jnp.float32
BF16 = jnp.bfloat16
HIGH = lax.Precision.HIGHEST

N_ROW = 8
N_COL = 16
DEVICES = N_ROW * N_COL
CYC = 128
CR = 256
CZ = 1024
EXT_R = 264
EXT_Z = 1152
SLOTS = 512
VISCOSITY = 0.2
CORE_SQUARE = 4.0
STEP_LENGTH = 4.0
CHUNK = 128


def iota(shape, dim):
    return lax.broadcasted_iota(jnp.int32, shape, dim)


def dot(a, b, contract, precision=None):
    return lax.dot_general(
        a, b, (contract, ((), ())), precision=precision, preferred_element_type=F32
    )


def halves(x):
    high = x.astype(BF16)
    return high, (x - high.astype(F32)).astype(BF16)


def dot3(a, b, contract):
    (ah, al), (bh, bl) = a, b
    ka, kb = contract[0][0], contract[1][0]
    left = jnp.concatenate([ah, ah, al], axis=ka)
    return dot(left, jnp.concatenate([bh, bl, bh], axis=kb), contract)


def tent(x):
    return jnp.maximum(1.0 - jnp.abs(x), 0.0)


def pair_terms(r, rr, z, a, a2, aa, src_z):
    d = z - src_z
    gap = a - r
    s = d * d + CORE_SQUARE
    near = s + gap * gap
    w = a2 * r
    u = near + w
    pq = (u + w) * near
    g = pq * lax.rsqrt(pq)
    b = g * lax.rsqrt(g)
    x = (u + g) * 0.5
    a = x * lax.rsqrt(x)
    t = []
    for _ in range(4):
        product = a * b
        t.append(product)
        a = (a + b) * 0.5
        b = product * lax.rsqrt(product)
    twice = a + b
    h = t[3]
    for n in (2, 1, 0):
        h = (h + h) + t[n]
    e = (8.0 * twice) * twice - ((h + h) + g)
    inverse = 1.0 / twice
    y = (e * inverse) * (1.0 / pq)
    radial = (u * y - inverse) * d
    even = inverse - y * s
    odd = y * (aa - rr)
    return radial, even + odd, even - odd


def kernel(
    cells_ref, offs_ref, stren_ref, btile_ref,
    disp_ref, diff_ref, renew_ref,
    src, ag, ret_send, ret_recv, tr, tz, tg, trr, acc_rad, acc_ax,
    out1, in1, out2, in2, zh, zl, ns_send, ns_recv, ew_send, ew_recv, co_send, co_recv, dep, fld,
    ag_ssem, ag_rsem, ret_sem, a1_sem, halo_ssem, halo_rsem, a2_sem,
):
    row = lax.axis_index("row")
    col = lax.axis_index("col")

    def at(kr, kc):
        return lax.rem(row + kr, N_ROW), lax.rem(col + kc, N_COL)

    def before(kr, kc):
        return lax.rem(row + (N_ROW - kr), N_ROW), lax.rem(col + (N_COL - kc), N_COL)

    segments = [
        (4, lambda i: 0, lambda i: 4 + i, True),
        (8, lambda i: 2, lambda i: i, True),
        (7, lambda i: 4, lambda i: 1 + i, True),
        (32, lambda i: 3 - 2 * (i // N_COL), lambda i: lax.rem(i, N_COL), True),
        (8, lambda i: 2, lambda i: 8 + i, True),
        (3, lambda i: 0, lambda i: 3 - i, True),
        (3, lambda i: 4 * ((i + 1) // 2), lambda i: 8 * (1 - i // 2), False),
    ]

    def over(segment, body):
        count, kr, kc, _ = segment

        def one(i, carry):
            body(kr(i), kc(i))
            return carry

        lax.fori_loop(0, count, one, 0)

    def each_shift(body):
        for segment in segments:
            over(segment, body)

    barrier = pltpu.get_barrier_semaphore()

    def greet(kr, kc):
        pl.semaphore_signal(barrier, inc=1, device_id=at(kr, kc), device_id_type=MESH)

    each_shift(greet)

    widen = (iota((64, CYC), 1) // 2 == iota((64, CYC), 0)).astype(F32)
    tile_of = dot(
        jnp.broadcast_to(btile_ref[...].astype(F32), (8, 64)), widen, ((1,), (0,)), HIGH
    )[0:1]
    tile_row = tile_of.astype(jnp.int32)
    part = tile_row & (N_COL - 1)
    slab = tile_row >> 4
    cell_r = jnp.clip(part * CR + cells_ref[0:1], 16, CR * N_COL - 3)
    cell_z = jnp.clip(slab * CZ + cells_ref[1:2], 2, CZ * N_ROW - 3)
    offs = offs_ref[...]
    pos_r = cell_r.astype(F32) + offs[0:1]
    pos_z = cell_z.astype(F32) + offs[1:2]
    strength = stren_ref[...]
    src[0:1] = pos_r
    src[1:2] = pos_z
    src[2:3] = (STEP_LENGTH * 0.5) * strength
    src[3:4] = jnp.zeros((1, CYC), F32)

    def column(v):
        return jnp.transpose(jnp.broadcast_to(v, (CYC, CYC)))

    tr[...] = column(pos_r)
    tz[...] = column(pos_z)
    tg[...] = column((STEP_LENGTH * 0.5) * strength)
    trr[...] = tr[...] * tr[...]
    acc_rad[...] = jnp.zeros((CYC, CYC), F32)
    acc_ax[...] = jnp.zeros((CYC, CYC), F32)

    def block(ref):
        a = ref[0:1, :]
        src_z = ref[1:2, :]
        src_g = ref[2:3, :]
        a, a2, aa, src_z, src_g = (
            jnp.broadcast_to(v, (CHUNK, CYC)) for v in (a, a + a, a * a, src_z, src_g)
        )
        back_rad = jnp.zeros((CHUNK, CYC), F32)
        back_ax = jnp.zeros((CHUNK, CYC), F32)
        for i in range(CYC // CHUNK):
            rows = pl.ds(i * CHUNK, CHUNK)
            radial, here, there = pair_terms(tr[rows], trr[rows], tz[rows], a, a2, aa, src_z)
            acc_rad[rows] += radial * src_g
            acc_ax[rows] += here * src_g
            own = tg[rows]
            back_rad += radial * own
            back_ax += there * own
        return back_rad, back_ax

    block(src)

    lane = iota((CYC, CYC), 1)
    sub = iota((CYC, CYC), 0)
    tile_rows = jnp.broadcast_to(tile_of, (CYC, CYC))
    same = (jnp.transpose(tile_rows) == tile_rows) & ((sub >> 1) < (lane >> 1))
    rank = jnp.sum(same.astype(F32), axis=0, keepdims=True)
    slot = rank.astype(jnp.int32) + (iota((1, CYC), 1) & 1)
    route = (sub == jnp.broadcast_to(tile_row, (CYC, CYC))).astype(F32)

    pl.semaphore_wait(barrier, 65)

    def send_source(kr, kc):
        pltpu.make_async_remote_copy(
            src_ref=src,
            dst_ref=ag.at[kr, kc],
            send_sem=ag_ssem,
            recv_sem=ag_rsem.at[kr, kc],
            device_id=before(kr, kc),
            device_id_type=MESH,
        ).start()

    each_shift(send_source)

    def arrive(kr, kc):
        pltpu.make_async_copy(src, ag.at[kr, kc], ag_rsem.at[kr, kc]).wait()

    def meet(kr, kc):
        back_rad, back_ax = block(ag.at[kr, kc])
        ret_send[kr, kc, 0:1] = jnp.sum(back_rad, axis=0, keepdims=True)
        ret_send[kr, kc, 1:2] = jnp.sum(back_ax, axis=0, keepdims=True)

    def send_back(kr, kc):
        pltpu.make_async_remote_copy(
            src_ref=ret_send.at[kr, kc],
            dst_ref=ret_recv.at[kr, kc],
            send_sem=ret_sem.at[0],
            recv_sem=ret_sem.at[1],
            device_id=at(kr, kc),
            device_id_type=MESH,
        ).start()

    def arrive_meet(kr, kc):
        arrive(kr, kc)
        meet(kr, kc)

    def full_meet(kr, kc):
        arrive_meet(kr, kc)
        send_back(kr, kc)

    for segment in segments:
        over(segment, full_meet if segment[-1] else arrive_meet)

    def wait_bytes(ref, count, sem):
        view = ref.at[pl.ds(0, count)]
        pltpu.make_async_copy(view, view, sem).wait()

    own_rad = jnp.sum(jnp.transpose(acc_rad[...]), axis=0, keepdims=True)
    own_ax = jnp.sum(jnp.transpose(acc_ax[...]), axis=0, keepdims=True)

    flat = ret_recv.reshape(5 * N_COL, 2, CYC)
    wait_bytes(flat, 62, ret_sem.at[1])
    got = jnp.sum(ret_recv[1:4], axis=(0, 1))
    got += jnp.sum(ret_recv[0, 1:8], axis=0) + jnp.sum(ret_recv[4, 1:8], axis=0)
    disp_r = (own_rad - got[0:1]) / pos_r
    disp_z = own_ax + got[1:2]
    disp_ref[0:1] = disp_r
    disp_ref[1:2] = disp_z

    moved_r = jnp.clip(offs[0:1] + disp_r, -1.0, 2.0)
    moved_z = jnp.clip(offs[1:2] + disp_z, -1.0, 2.0)
    local_r = (cell_r - part * CR).astype(F32)
    local_z = (cell_z - slab * CZ).astype(F32)
    blank = jnp.zeros((3, CYC), F32)
    values = jnp.concatenate([local_r, moved_r, local_z, moved_z, strength, blank], axis=0)
    payload = jnp.concatenate([jnp.where(slot == s, values, 0.0) for s in range(4)], axis=0)
    payload = jnp.concatenate([payload, jnp.zeros((96, CYC), F32)], axis=0)
    out1[:, 0, :] = dot(route, payload, ((1,), (1,)), HIGH)

    me = row * N_COL + col

    def to_all(out, into, sem):
        def outer(i, carry):
            kr = lax.rem(3 * i + 3, N_ROW)
            dr = lax.rem(row + kr, N_ROW)

            def send(dc):
                pltpu.make_async_remote_copy(
                    src_ref=out.at[dr * N_COL + dc],
                    dst_ref=into.at[me],
                    send_sem=sem.at[0],
                    recv_sem=sem.at[1],
                    device_id=(dr, dc),
                    device_id_type=MESH,
                ).start()

            for kc in range(1, N_COL):
                send(lax.rem(col + kc, N_COL))

            @pl.when(kr > 0)
            def _():
                send(col)

            return carry

        lax.fori_loop(0, N_ROW, outer, 0)
        into[me] = out[me]
        wait_bytes(into, DEVICES - 1, sem.at[1])

    to_all(out1, in1, a1_sem)

    across = jnp.transpose(in1[:, 0, :])

    def spread(value):
        return jnp.concatenate([across[8 * s + value : 8 * s + value + 1] for s in range(4)], axis=1)

    cell_r4, moved_r4, cell_z4, moved_z4, power = (spread(v) for v in range(5))
    wrapped = iota((16, SLOTS), 0) & 7
    wrapped = wrapped - jnp.where(wrapped < 4, 0, 8)
    first = iota((16, SLOTS), 0) < 8
    edge_z = tent(((wrapped + jnp.where(first, CZ, 0)).astype(F32) - cell_z4) - moved_z4)
    edge_r = tent(((wrapped + jnp.where(first, CR, 0)).astype(F32) - cell_r4) - moved_r4) * power
    edge_z, edge_r = halves(edge_z), halves(edge_r)
    corners = dot3(edge_z, edge_r, ((1,), (1,)))
    corners = jnp.concatenate([corners, jnp.zeros((16, 112), F32)], axis=1)
    co_send[0] = corners[0:8]
    co_send[1] = corners[8:16]

    next_r, prev_r = lax.rem(row + 1, N_ROW), lax.rem(row + N_ROW - 1, N_ROW)
    next_c, prev_c = lax.rem(col + 1, N_COL), lax.rem(col + N_COL - 1, N_COL)
    copies = []

    def give(source, target, device):
        i = len(copies)
        copy = pltpu.make_async_remote_copy(
            src_ref=source,
            dst_ref=target,
            send_sem=halo_ssem.at[i],
            recv_sem=halo_rsem.at[i],
            device_id=device,
            device_id_type=MESH,
        )
        copy.start()
        copies.append(copy)

    give(co_send.at[0], co_recv.at[0], (next_r, next_c))
    give(co_send.at[0], co_recv.at[1], (next_r, prev_c))
    give(co_send.at[1], co_recv.at[2], (prev_r, next_c))
    give(co_send.at[1], co_recv.at[3], (prev_r, prev_c))

    step = iota((EXT_R, SLOTS), 0)
    cell_of_row = jnp.where(step < 260, step, step - EXT_R).astype(F32)
    radial = tent((cell_of_row - cell_r4) - moved_r4)
    loaded_h, loaded_l = halves(radial * power)
    strips = dot3(edge_z, (loaded_h, loaded_l), ((1,), (1,)))
    strips = jnp.concatenate([strips, jnp.zeros((16, 384 - EXT_R), F32)], axis=1)
    ew_send[0] = strips[0:8]
    ew_send[1] = strips[8:16]
    give(ew_send.at[0], ew_recv.at[0], (next_r, col))
    give(ew_send.at[1], ew_recv.at[1], (prev_r, col))

    def axial(i, carry):
        start = jnp.where(i < 34, i * 32, i * 32 - EXT_Z)
        cell = (iota((32, SLOTS), 0) + start).astype(F32)
        high, low = halves(tent((cell - cell_z4) - moved_z4))
        rows = pl.ds(pl.multiple_of(i * 32, 32), 32)
        zh[rows] = high
        zl[rows] = low
        return carry

    lax.fori_loop(0, EXT_Z // 32, axial, 0, unroll=1)
    weights = (zh[...], zl[...])
    loaded = tuple(jnp.concatenate(pair, axis=0) for pair in zip((loaded_h, loaded_l), edge_r))
    both = dot3(loaded, weights, ((1,), (1,)))
    ns_send[0] = both[EXT_R : EXT_R + 8]
    ns_send[1] = both[EXT_R + 8 :]
    give(ns_send.at[0], ns_recv.at[0], (row, next_c))
    give(ns_send.at[1], ns_recv.at[1], (row, prev_c))
    dep[...] = both[:EXT_R]

    base = col * CR

    def viscous(i, window, keep):
        cut = (lambda x: x) if keep is None else (lambda x: x[:, keep[0] : keep[1]])
        load = lambda k: window(pl.ds(8 * (k % (EXT_R // 8)), 8))
        wide = load(i)
        width = wide.shape[1]
        here = cut(wide)
        inward = jnp.concatenate([cut(load(i - 1))[7:8], here[0:7]], axis=0)
        outward = jnp.concatenate([here[1:8], cut(load(i + 1))[0:1]], axis=0)
        forward = cut(pltpu.roll(wide, width - 1, axis=1))
        backward = cut(pltpu.roll(wide, 1, axis=1))
        number = iota((8, 128), 0) + 8 * i
        number = jnp.where(number < 260, number, number - EXT_R) + base
        radius = jnp.maximum(number, 1).astype(F32)
        count = here.shape[1] // 128
        half = jnp.concatenate([0.5 / radius] * count, axis=1)
        square = jnp.concatenate([1.0 / (radius * radius)] * count, axis=1)
        laplace = (
            (outward + inward)
            + (forward + backward)
            - 4.0 * here
            + (outward - inward) * half
            - here * square
        )
        return here + VISCOSITY * laplace

    inner = range(1, CR // 8 - 1)
    for i in inner:
        new = viscous(i, lambda rows: dep[rows, 0:1024], (128, 896))
        fld[8 * i : 8 * i + 8, 128:896] = new
        diff_ref[8 * i : 8 * i + 8, 128:896] = new

    for copy in copies:
        copy.wait_recv()

    has_next_r, has_prev_r = row < N_ROW - 1, row > 0
    has_next_c, has_prev_c = col < N_COL - 1, col > 0
    strip_lane = iota((8, CYC), 1)

    def side(i, present):
        wide = jnp.where(present, ew_recv[i], 0.0)
        first, second, third = wide[:, 0:128], wide[:, 128:256], wide[:, 256:384]
        third = jnp.where(strip_lane < 8, third, 0.0)
        low = jnp.where(has_prev_c & present, co_recv[2 * i], 0.0)
        high = jnp.where(has_next_c & present, co_recv[2 * i + 1], 0.0)
        first += jnp.where(strip_lane < 4, low, 0.0)
        third += jnp.where((strip_lane >= 4) & (strip_lane < 8), low, 0.0)
        third += jnp.where(strip_lane < 4, pltpu.roll(high, 120, axis=1), 0.0)
        second += jnp.where(strip_lane >= 124, pltpu.roll(high, 112, axis=1), 0.0)
        wide = jnp.concatenate([first, second, third], axis=1)
        upper = iota((8, 384), 0) < 4
        wide = jnp.concatenate(
            [jnp.where(upper, wide, 0.0), jnp.zeros((112, 384), F32), jnp.where(upper, 0.0, wide)],
            axis=0,
        )
        return jnp.transpose(wide)[0:EXT_R]

    left = side(0, has_prev_r)
    right = side(1, has_next_r)
    front = iota((EXT_R, 128), 1) < 64
    dep[:, 0:128] += jnp.where(front, left, 0.0)
    dep[:, 896:1024] += jnp.where(front, 0.0, right)
    dep[:, 1024:1152] += jnp.where(front, right, left)
    upper = iota((8, EXT_Z), 0) < 4
    above = jnp.where(has_prev_c, ns_recv[0], 0.0)
    below = jnp.where(has_next_c, ns_recv[1], 0.0)
    dep[0:8] += jnp.where(upper, above, 0.0)
    dep[248:256] += jnp.where(upper, 0.0, below)
    dep[256:264] += jnp.where(upper, below, above)

    for i in (0, CR // 8 - 1, CR // 8):
        new = viscous(i, lambda rows: dep[rows], None)
        fld[8 * i : 8 * i + 8] = new
        if i < CR // 8:
            diff_ref[8 * i : 8 * i + 8] = new[:, 0:CZ]
    for i in inner:
        new = viscous(
            i,
            lambda rows: jnp.concatenate([dep[rows, 768:1152], dep[rows, 0:256]], axis=1),
            (128, 512),
        )
        fld[8 * i : 8 * i + 8, 896:1152] = new[:, 0:256]
        fld[8 * i : 8 * i + 8, 0:128] = new[:, 256:384]
        diff_ref[8 * i : 8 * i + 8, 896:1024] = new[:, 0:128]
        diff_ref[8 * i : 8 * i + 8, 0:128] = new[:, 256:384]

    read = dot3(halves(fld[...]), (zh[...], zl[...]), ((1,), (0,)))
    found = jnp.sum(read * radial, axis=0, keepdims=True)
    found = jnp.concatenate(
        [found[:, CYC * s : CYC * s + CYC] for s in range(4)] + [jnp.zeros((124, CYC), F32)], axis=0
    )
    out2[:, 0, :] = jnp.transpose(found)
    to_all(out2, in2, a2_sem)
    table = jnp.transpose(in2[:, 0, :])[0:8]
    mine = dot(table, route, ((1,), (0,)), HIGH)
    renew_ref[...] = jnp.sum(
        jnp.where(iota((8, CYC), 0) == slot, mine, 0.0), axis=0, keepdims=True
    )

    sent = ag.reshape(5 * N_COL, 4, CYC)
    wait_bytes(sent, 65, ag_ssem)
    wait_bytes(flat, 62, ret_sem.at[0])
    wait_bytes(out1, DEVICES - 1, a1_sem.at[0])
    wait_bytes(out2, DEVICES - 1, a2_sem.at[0])
    for copy in copies:
        copy.wait_send()


def write_out(disp_ref, diff_ref, renew_ref, disp_out, diff_out, renew_out, sem):
    pairs = [(disp_ref, disp_out), (renew_ref, renew_out)]
    for i in range(8):
        rows = pl.ds(i * CR // 8, CR // 8)
        pairs.append((diff_ref.at[rows], diff_out.at[rows]))
    copies = [
        pltpu.make_async_copy(source, target, sem.at[i])
        for i, (source, target) in enumerate(pairs)
    ]
    for copy in copies:
        copy.start()
    for copy in copies:
        copy.wait()


def on_device(cycle_cells, cycle_offsets, cycle_strength, block_tile):
    vmem = pl.BlockSpec(memory_space=pltpu.VMEM)
    hbm = pl.BlockSpec(memory_space=pl.ANY)
    dma = pltpu.SemaphoreType.DMA
    shapes = [
        jax.ShapeDtypeStruct((2, CYC), F32),
        jax.ShapeDtypeStruct((CR, CZ), F32),
        jax.ShapeDtypeStruct((1, CYC), F32),
    ]
    results = pl.pallas_call(
        kernel,
        out_shape=shapes,
        in_specs=[vmem] * 4,
        out_specs=[vmem] * 3,
        scratch_shapes=[
            pltpu.VMEM((4, CYC), F32),
            pltpu.VMEM((5, N_COL, 4, CYC), F32),
            pltpu.VMEM((5, N_COL, 2, CYC), F32),
            pltpu.VMEM((5, N_COL, 2, CYC), F32),
            pltpu.VMEM((CYC, CYC), F32),
            pltpu.VMEM((CYC, CYC), F32),
            pltpu.VMEM((CYC, CYC), F32),
            pltpu.VMEM((CYC, CYC), F32),
            pltpu.VMEM((CYC, CYC), F32),
            pltpu.VMEM((CYC, CYC), F32),
            pltpu.VMEM((DEVICES, 1, CYC), F32),
            pltpu.VMEM((DEVICES, 1, CYC), F32),
            pltpu.VMEM((DEVICES, 1, CYC), F32),
            pltpu.VMEM((DEVICES, 1, CYC), F32),
            pltpu.VMEM((EXT_Z, SLOTS), BF16),
            pltpu.VMEM((EXT_Z, SLOTS), BF16),
            pltpu.VMEM((2, 8, EXT_Z), F32),
            pltpu.VMEM((2, 8, EXT_Z), F32),
            pltpu.VMEM((2, 8, 384), F32),
            pltpu.VMEM((2, 8, 384), F32),
            pltpu.VMEM((2, 8, 128), F32),
            pltpu.VMEM((4, 8, 128), F32),
            pltpu.VMEM((EXT_R, EXT_Z), F32),
            pltpu.VMEM((EXT_R, EXT_Z), F32),
            dma,
            dma((5, N_COL)),
            dma((2,)),
            dma((2,)),
            dma((8,)),
            dma((8,)),
            dma((2,)),
        ],
        compiler_params=pltpu.CompilerParams(
            collective_id=0, has_side_effects=True, vmem_limit_bytes=40 * 2**20
        ),
    )(cycle_cells, cycle_offsets, cycle_strength.reshape(1, CYC), block_tile.reshape(1, -1))
    displacement, diffused, renewed = pl.pallas_call(
        write_out,
        out_shape=shapes,
        in_specs=[vmem] * 3,
        out_specs=[hbm] * 3,
        scratch_shapes=[dma((10,))],
        compiler_params=pltpu.CompilerParams(vmem_limit_bytes=2**20),
    )(*results)
    return displacement, diffused, renewed.reshape(CYC)


def solution(mesh):
    in_specs = (
        P(None, ("row", "col")),
        P(None, ("row", "col")),
        P(("row", "col")),
        P(("row", "col")),
    )
    out_specs = (P(None, ("row", "col")), P("col", "row"), P(("row", "col")))
    return jax.shard_map(
        on_device, mesh=mesh, in_specs=in_specs, out_specs=out_specs, check_vma=False
    )
```

```python
import jax
import jax.numpy as jnp
from jax import lax
from jax.experimental import pallas as pl
from jax.experimental.pallas import tpu as pltpu
from jax.sharding import PartitionSpec as P

MESH = pl.DeviceIdType.MESH
F32 = jnp.float32
BF16 = jnp.bfloat16
HIGH = lax.Precision.HIGHEST

N_ROW = 8
N_COL = 16
DEVICES = N_ROW * N_COL
CYC = 128
CR = 256
CZ = 1024
EXT_R = 264
EXT_Z = 1152
SLOTS = 512
VISCOSITY = 0.2
CORE_SQUARE = 4.0
STEP_LENGTH = 4.0
CHUNK = 128


def iota(shape, dim):
    return lax.broadcasted_iota(jnp.int32, shape, dim)


def dot(a, b, contract, precision=None):
    return lax.dot_general(
        a, b, (contract, ((), ())), precision=precision, preferred_element_type=F32
    )


def halves(x):
    high = x.astype(BF16)
    return high, (x - high.astype(F32)).astype(BF16)


def dot3(a, b, contract):
    (ah, al), (bh, bl) = a, b
    ka, kb = contract[0][0], contract[1][0]
    left = jnp.concatenate([ah, ah, al], axis=ka)
    return dot(left, jnp.concatenate([bh, bl, bh], axis=kb), contract)


def tent(x):
    return jnp.maximum(1.0 - jnp.abs(x), 0.0)


def pair_terms(r, rr, z, a, a2, aa, src_z):
    d = z - src_z
    gap = a - r
    s = d * d + CORE_SQUARE
    near = s + gap * gap
    w = a2 * r
    u = near + w
    pq = (u + w) * near
    g = pq * lax.rsqrt(pq)
    b = g * lax.rsqrt(g)
    x = (u + g) * 0.5
    a = x * lax.rsqrt(x)
    t = []
    for _ in range(4):
        product = a * b
        t.append(product)
        a = (a + b) * 0.5
        b = product * lax.rsqrt(product)
    twice = a + b
    h = t[3]
    for n in (2, 1, 0):
        h = (h + h) + t[n]
    e = (8.0 * twice) * twice - ((h + h) + g)
    inverse = 1.0 / twice
    y = (e * inverse) * (1.0 / pq)
    radial = (u * y - inverse) * d
    even = inverse - y * s
    odd = y * (aa - rr)
    return radial, even + odd, even - odd


def kernel(
    cells_ref, offs_ref, stren_ref, btile_ref,
    disp_ref, diff_ref, renew_ref,
    src, ag, ret_send, ret_recv, tr, tz, tg, trr, acc_rad, acc_ax,
    out1, in1, out2, in2, zh, zl, ns_send, ns_recv, ew_send, ew_recv, co_send, co_recv, dep, fld,
    ag_ssem, ag_rsem, ret_sem, a1_sem, halo_ssem, halo_rsem, a2_sem,
):
    row = lax.axis_index("row")
    col = lax.axis_index("col")

    def at(kr, kc):
        return lax.rem(row + kr, N_ROW), lax.rem(col + kc, N_COL)

    def before(kr, kc):
        return lax.rem(row + (N_ROW - kr), N_ROW), lax.rem(col + (N_COL - kc), N_COL)

    segments = [
        (4, lambda i: 0, lambda i: 4 + i, True),
        (8, lambda i: 2, lambda i: i, True),
        (7, lambda i: 4, lambda i: 1 + i, True),
        (32, lambda i: 3 - 2 * (i // N_COL), lambda i: lax.rem(i, N_COL), True),
        (8, lambda i: 2, lambda i: 8 + i, True),
        (3, lambda i: 0, lambda i: 3 - i, True),
        (3, lambda i: 4 * ((i + 1) // 2), lambda i: 8 * (1 - i // 2), False),
    ]

    def over(segment, body):
        count, kr, kc, _ = segment

        def one(i, carry):
            body(kr(i), kc(i))
            return carry

        lax.fori_loop(0, count, one, 0)

    def each_shift(body):
        for segment in segments:
            over(segment, body)

    barrier = pltpu.get_barrier_semaphore()

    def greet(kr, kc):
        pl.semaphore_signal(barrier, inc=1, device_id=at(kr, kc), device_id_type=MESH)

    for segment in reversed(segments):
        over(segment, greet)

    widen = (iota((64, CYC), 1) // 2 == iota((64, CYC), 0)).astype(F32)
    tile_of = dot(
        jnp.broadcast_to(btile_ref[...].astype(F32), (8, 64)), widen, ((1,), (0,)), HIGH
    )[0:1]
    tile_row = tile_of.astype(jnp.int32)
    part = tile_row & (N_COL - 1)
    slab = tile_row >> 4
    cell_r = jnp.clip(part * CR + cells_ref[0:1], 16, CR * N_COL - 3)
    cell_z = jnp.clip(slab * CZ + cells_ref[1:2], 2, CZ * N_ROW - 3)
    offs = offs_ref[...]
    pos_r = cell_r.astype(F32) + offs[0:1]
    pos_z = cell_z.astype(F32) + offs[1:2]
    strength = stren_ref[...]
    src[0:1] = pos_r
    src[1:2] = pos_z
    src[2:3] = (STEP_LENGTH * 0.5) * strength
    src[3:4] = jnp.zeros((1, CYC), F32)

    def column(v):
        return jnp.transpose(jnp.broadcast_to(v, (CYC, CYC)))

    tr[...] = column(pos_r)
    tz[...] = column(pos_z)
    tg[...] = column((STEP_LENGTH * 0.5) * strength)
    trr[...] = tr[...] * tr[...]
    acc_rad[...] = jnp.zeros((CYC, CYC), F32)
    acc_ax[...] = jnp.zeros((CYC, CYC), F32)

    def block(ref):
        a = ref[0:1, :]
        src_z = ref[1:2, :]
        src_g = ref[2:3, :]
        a, a2, aa, src_z, src_g = (
            jnp.broadcast_to(v, (CHUNK, CYC)) for v in (a, a + a, a * a, src_z, src_g)
        )
        back_rad = jnp.zeros((CHUNK, CYC), F32)
        back_ax = jnp.zeros((CHUNK, CYC), F32)
        for i in range(CYC // CHUNK):
            rows = pl.ds(i * CHUNK, CHUNK)
            radial, here, there = pair_terms(tr[rows], trr[rows], tz[rows], a, a2, aa, src_z)
            acc_rad[rows] += radial * src_g
            acc_ax[rows] += here * src_g
            own = tg[rows]
            back_rad += radial * own
            back_ax += there * own
        return back_rad, back_ax

    block(src)

    lane = iota((CYC, CYC), 1)
    sub = iota((CYC, CYC), 0)
    tile_rows = jnp.broadcast_to(tile_of, (CYC, CYC))
    same = (jnp.transpose(tile_rows) == tile_rows) & ((sub >> 1) < (lane >> 1))
    rank = jnp.sum(same.astype(F32), axis=0, keepdims=True)
    slot = rank.astype(jnp.int32) + (iota((1, CYC), 1) & 1)
    route = (sub == jnp.broadcast_to(tile_row, (CYC, CYC))).astype(F32)

    pl.semaphore_wait(barrier, 65)

    def send_source(kr, kc):
        pltpu.make_async_remote_copy(
            src_ref=src,
            dst_ref=ag.at[kr, kc],
            send_sem=ag_ssem,
            recv_sem=ag_rsem.at[kr, kc],
            device_id=before(kr, kc),
            device_id_type=MESH,
        ).start()

    each_shift(send_source)

    def arrive(kr, kc):
        pltpu.make_async_copy(src, ag.at[kr, kc], ag_rsem.at[kr, kc]).wait()

    def meet(kr, kc):
        back_rad, back_ax = block(ag.at[kr, kc])
        ret_send[kr, kc, 0:1] = jnp.sum(back_rad, axis=0, keepdims=True)
        ret_send[kr, kc, 1:2] = jnp.sum(back_ax, axis=0, keepdims=True)

    def send_back(kr, kc):
        pltpu.make_async_remote_copy(
            src_ref=ret_send.at[kr, kc],
            dst_ref=ret_recv.at[kr, kc],
            send_sem=ret_sem.at[0],
            recv_sem=ret_sem.at[1],
            device_id=at(kr, kc),
            device_id_type=MESH,
        ).start()

    def arrive_meet(kr, kc):
        arrive(kr, kc)
        meet(kr, kc)

    def full_meet(kr, kc):
        arrive_meet(kr, kc)
        send_back(kr, kc)

    for segment in segments:
        over(segment, full_meet if segment[-1] else arrive_meet)

    def wait_bytes(ref, count, sem):
        view = ref.at[pl.ds(0, count)]
        pltpu.make_async_copy(view, view, sem).wait()

    own_rad = jnp.sum(jnp.transpose(acc_rad[...]), axis=0, keepdims=True)
    own_ax = jnp.sum(jnp.transpose(acc_ax[...]), axis=0, keepdims=True)

    flat = ret_recv.reshape(5 * N_COL, 2, CYC)
    wait_bytes(flat, 62, ret_sem.at[1])
    got = jnp.sum(ret_recv[1:4], axis=(0, 1))
    got += jnp.sum(ret_recv[0, 1:8], axis=0) + jnp.sum(ret_recv[4, 1:8], axis=0)
    disp_r = (own_rad - got[0:1]) / pos_r
    disp_z = own_ax + got[1:2]
    disp_ref[0:1] = disp_r
    disp_ref[1:2] = disp_z

    moved_r = jnp.clip(offs[0:1] + disp_r, -1.0, 2.0)
    moved_z = jnp.clip(offs[1:2] + disp_z, -1.0, 2.0)
    local_r = (cell_r - part * CR).astype(F32)
    local_z = (cell_z - slab * CZ).astype(F32)
    blank = jnp.zeros((3, CYC), F32)
    values = jnp.concatenate([local_r, moved_r, local_z, moved_z, strength, blank], axis=0)
    payload = jnp.concatenate([jnp.where(slot == s, values, 0.0) for s in range(4)], axis=0)
    out1[:, 0, :] = jnp.concatenate(
        [dot(route, payload, ((1,), (1,)), HIGH), jnp.zeros((CYC, 96), F32)], axis=1
    )

    me = row * N_COL + col

    def to_all(out, into, sem):
        def outer(i, carry):
            kr = lax.rem(3 * i + 3, N_ROW)
            dr = lax.rem(row + kr, N_ROW)

            def send(dc):
                pltpu.make_async_remote_copy(
                    src_ref=out.at[dr * N_COL + dc],
                    dst_ref=into.at[me],
                    send_sem=sem.at[0],
                    recv_sem=sem.at[1],
                    device_id=(dr, dc),
                    device_id_type=MESH,
                ).start()

            for kc in range(1, N_COL):
                send(lax.rem(col + kc, N_COL))

            @pl.when(kr > 0)
            def _():
                send(col)

            return carry

        lax.fori_loop(0, N_ROW, outer, 0)
        into[me] = out[me]
        wait_bytes(into, DEVICES - 1, sem.at[1])

    to_all(out1, in1, a1_sem)

    across = jnp.transpose(in1[:, 0, :])

    def spread(value):
        return jnp.concatenate([across[8 * s + value : 8 * s + value + 1] for s in range(4)], axis=1)

    cell_r4, moved_r4, cell_z4, moved_z4, power = (spread(v) for v in range(5))
    wrapped = iota((16, SLOTS), 0) & 7
    wrapped = wrapped - jnp.where(wrapped < 4, 0, 8)
    first = iota((16, SLOTS), 0) < 8
    edge_z = tent(((wrapped + jnp.where(first, CZ, 0)).astype(F32) - cell_z4) - moved_z4)
    edge_r = tent(((wrapped + jnp.where(first, CR, 0)).astype(F32) - cell_r4) - moved_r4) * power
    edge_z, edge_r = halves(edge_z), halves(edge_r)
    corners = dot3(edge_z, edge_r, ((1,), (1,)))
    corners = jnp.concatenate([corners, jnp.zeros((16, 112), F32)], axis=1)
    co_send[0] = corners[0:8]
    co_send[1] = corners[8:16]

    next_r, prev_r = lax.rem(row + 1, N_ROW), lax.rem(row + N_ROW - 1, N_ROW)
    next_c, prev_c = lax.rem(col + 1, N_COL), lax.rem(col + N_COL - 1, N_COL)
    copies = []

    def give(source, target, device):
        i = len(copies)
        copy = pltpu.make_async_remote_copy(
            src_ref=source,
            dst_ref=target,
            send_sem=halo_ssem.at[i],
            recv_sem=halo_rsem.at[i],
            device_id=device,
            device_id_type=MESH,
        )
        copy.start()
        copies.append(copy)

    give(co_send.at[0], co_recv.at[0], (next_r, next_c))
    give(co_send.at[0], co_recv.at[1], (next_r, prev_c))
    give(co_send.at[1], co_recv.at[2], (prev_r, next_c))
    give(co_send.at[1], co_recv.at[3], (prev_r, prev_c))

    step = iota((EXT_R, SLOTS), 0)
    cell_of_row = jnp.where(step < 260, step, step - EXT_R).astype(F32)
    radial = tent((cell_of_row - cell_r4) - moved_r4)
    loaded_h, loaded_l = halves(radial * power)
    strips = dot3(edge_z, (loaded_h, loaded_l), ((1,), (1,)))
    strips = jnp.concatenate([strips, jnp.zeros((16, 384 - EXT_R), F32)], axis=1)
    ew_send[0] = strips[0:8]
    ew_send[1] = strips[8:16]
    give(ew_send.at[0], ew_recv.at[0], (next_r, col))
    give(ew_send.at[1], ew_recv.at[1], (prev_r, col))

    def axial(i, carry):
        start = jnp.where(i < 34, i * 32, i * 32 - EXT_Z)
        cell = (iota((32, SLOTS), 0) + start).astype(F32)
        high, low = halves(tent((cell - cell_z4) - moved_z4))
        rows = pl.ds(pl.multiple_of(i * 32, 32), 32)
        zh[rows] = high
        zl[rows] = low
        return carry

    lax.fori_loop(0, EXT_Z // 32, axial, 0, unroll=1)
    weights = (zh[...], zl[...])
    loaded = tuple(jnp.concatenate(pair, axis=0) for pair in zip((loaded_h, loaded_l), edge_r))
    both = dot3(loaded, weights, ((1,), (1,)))
    ns_send[0] = both[EXT_R : EXT_R + 8]
    ns_send[1] = both[EXT_R + 8 :]
    give(ns_send.at[0], ns_recv.at[0], (row, next_c))
    give(ns_send.at[1], ns_recv.at[1], (row, prev_c))
    dep[...] = both[:EXT_R]

    base = col * CR

    def viscous(i, window, keep):
        cut = (lambda x: x) if keep is None else (lambda x: x[:, keep[0] : keep[1]])
        load = lambda k: window(pl.ds(8 * (k % (EXT_R // 8)), 8))
        wide = load(i)
        width = wide.shape[1]
        here = cut(wide)
        inward = jnp.concatenate([cut(load(i - 1))[7:8], here[0:7]], axis=0)
        outward = jnp.concatenate([here[1:8], cut(load(i + 1))[0:1]], axis=0)
        forward = cut(pltpu.roll(wide, width - 1, axis=1))
        backward = cut(pltpu.roll(wide, 1, axis=1))
        number = iota((8, 128), 0) + 8 * i
        number = jnp.where(number < 260, number, number - EXT_R) + base
        radius = jnp.maximum(number, 1).astype(F32)
        count = here.shape[1] // 128
        half = jnp.concatenate([0.5 / radius] * count, axis=1)
        square = jnp.concatenate([1.0 / (radius * radius)] * count, axis=1)
        laplace = (
            (outward + inward)
            + (forward + backward)
            - 4.0 * here
            + (outward - inward) * half
            - here * square
        )
        return here + VISCOSITY * laplace

    inner = range(1, CR // 8 - 1)
    for i in inner:
        new = viscous(i, lambda rows: dep[rows, 0:1024], (128, 896))
        fld[8 * i : 8 * i + 8, 128:896] = new
        diff_ref[8 * i : 8 * i + 8, 128:896] = new

    for copy in copies:
        copy.wait_recv()

    has_next_r, has_prev_r = row < N_ROW - 1, row > 0
    has_next_c, has_prev_c = col < N_COL - 1, col > 0
    strip_lane = iota((8, CYC), 1)

    def side(i, present):
        wide = jnp.where(present, ew_recv[i], 0.0)
        first, second, third = wide[:, 0:128], wide[:, 128:256], wide[:, 256:384]
        third = jnp.where(strip_lane < 8, third, 0.0)
        low = jnp.where(has_prev_c & present, co_recv[2 * i], 0.0)
        high = jnp.where(has_next_c & present, co_recv[2 * i + 1], 0.0)
        first += jnp.where(strip_lane < 4, low, 0.0)
        third += jnp.where((strip_lane >= 4) & (strip_lane < 8), low, 0.0)
        third += jnp.where(strip_lane < 4, pltpu.roll(high, 120, axis=1), 0.0)
        second += jnp.where(strip_lane >= 124, pltpu.roll(high, 112, axis=1), 0.0)
        wide = jnp.concatenate([first, second, third], axis=1)
        upper = iota((8, 384), 0) < 4
        wide = jnp.concatenate(
            [jnp.where(upper, wide, 0.0), jnp.zeros((112, 384), F32), jnp.where(upper, 0.0, wide)],
            axis=0,
        )
        return jnp.transpose(wide)[0:EXT_R]

    left = side(0, has_prev_r)
    right = side(1, has_next_r)
    front = iota((EXT_R, 128), 1) < 64
    dep[:, 0:128] += jnp.where(front, left, 0.0)
    dep[:, 896:1024] += jnp.where(front, 0.0, right)
    dep[:, 1024:1152] += jnp.where(front, right, left)
    upper = iota((8, EXT_Z), 0) < 4
    above = jnp.where(has_prev_c, ns_recv[0], 0.0)
    below = jnp.where(has_next_c, ns_recv[1], 0.0)
    dep[0:8] += jnp.where(upper, above, 0.0)
    dep[248:256] += jnp.where(upper, 0.0, below)
    dep[256:264] += jnp.where(upper, below, above)

    for i in (0, CR // 8 - 1, CR // 8):
        new = viscous(i, lambda rows: dep[rows], None)
        fld[8 * i : 8 * i + 8] = new
        if i < CR // 8:
            diff_ref[8 * i : 8 * i + 8] = new[:, 0:CZ]
    for i in inner:
        new = viscous(
            i,
            lambda rows: jnp.concatenate([dep[rows, 768:1152], dep[rows, 0:256]], axis=1),
            (128, 512),
        )
        fld[8 * i : 8 * i + 8, 896:1152] = new[:, 0:256]
        fld[8 * i : 8 * i + 8, 0:128] = new[:, 256:384]
        diff_ref[8 * i : 8 * i + 8, 896:1024] = new[:, 0:128]
        diff_ref[8 * i : 8 * i + 8, 0:128] = new[:, 256:384]

    read = dot3(halves(fld[...]), (zh[...], zl[...]), ((1,), (0,)))
    found = jnp.sum(read * radial, axis=0, keepdims=True)
    found = jnp.concatenate(
        [found[:, CYC * s : CYC * s + CYC] for s in range(4)] + [jnp.zeros((124, CYC), F32)], axis=0
    )
    out2[:, 0, :] = jnp.transpose(found)
    to_all(out2, in2, a2_sem)
    table = jnp.transpose(in2[:, 0, :])[0:8]
    mine = dot(table, route, ((1,), (0,)), HIGH)
    renew_ref[...] = jnp.sum(
        jnp.where(iota((8, CYC), 0) == slot, mine, 0.0), axis=0, keepdims=True
    )

    sent = ag.reshape(5 * N_COL, 4, CYC)
    wait_bytes(sent, 65, ag_ssem)
    wait_bytes(flat, 62, ret_sem.at[0])
    wait_bytes(out1, DEVICES - 1, a1_sem.at[0])
    wait_bytes(out2, DEVICES - 1, a2_sem.at[0])
    for copy in copies:
        copy.wait_send()


def write_out(disp_ref, diff_ref, renew_ref, disp_out, diff_out, renew_out, sem):
    pairs = [(disp_ref, disp_out), (renew_ref, renew_out)]
    for i in range(2):
        rows = pl.ds(i * CR // 2, CR // 2)
        pairs.append((diff_ref.at[rows], diff_out.at[rows]))
    copies = [
        pltpu.make_async_copy(source, target, sem.at[i])
        for i, (source, target) in enumerate(pairs)
    ]
    for copy in copies:
        copy.start()
    for copy in copies:
        copy.wait()


def on_device(cycle_cells, cycle_offsets, cycle_strength, block_tile):
    vmem = pl.BlockSpec(memory_space=pltpu.VMEM)
    hbm = pl.BlockSpec(memory_space=pl.ANY)
    dma = pltpu.SemaphoreType.DMA
    shapes = [
        jax.ShapeDtypeStruct((2, CYC), F32),
        jax.ShapeDtypeStruct((CR, CZ), F32),
        jax.ShapeDtypeStruct((1, CYC), F32),
    ]
    results = pl.pallas_call(
        kernel,
        out_shape=shapes,
        in_specs=[vmem] * 4,
        out_specs=[vmem] * 3,
        scratch_shapes=[
            pltpu.VMEM((4, CYC), F32),
            pltpu.VMEM((5, N_COL, 4, CYC), F32),
            pltpu.VMEM((5, N_COL, 2, CYC), F32),
            pltpu.VMEM((5, N_COL, 2, CYC), F32),
            pltpu.VMEM((CYC, CYC), F32),
            pltpu.VMEM((CYC, CYC), F32),
            pltpu.VMEM((CYC, CYC), F32),
            pltpu.VMEM((CYC, CYC), F32),
            pltpu.VMEM((CYC, CYC), F32),
            pltpu.VMEM((CYC, CYC), F32),
            pltpu.VMEM((DEVICES, 1, CYC), F32),
            pltpu.VMEM((DEVICES, 1, CYC), F32),
            pltpu.VMEM((DEVICES, 1, CYC), F32),
            pltpu.VMEM((DEVICES, 1, CYC), F32),
            pltpu.VMEM((EXT_Z, SLOTS), BF16),
            pltpu.VMEM((EXT_Z, SLOTS), BF16),
            pltpu.VMEM((2, 8, EXT_Z), F32),
            pltpu.VMEM((2, 8, EXT_Z), F32),
            pltpu.VMEM((2, 8, 384), F32),
            pltpu.VMEM((2, 8, 384), F32),
            pltpu.VMEM((2, 8, 128), F32),
            pltpu.VMEM((4, 8, 128), F32),
            pltpu.VMEM((EXT_R, EXT_Z), F32),
            pltpu.VMEM((EXT_R, EXT_Z), F32),
            dma,
            dma((5, N_COL)),
            dma((2,)),
            dma((2,)),
            dma((8,)),
            dma((8,)),
            dma((2,)),
        ],
        compiler_params=pltpu.CompilerParams(
            collective_id=0, has_side_effects=True, vmem_limit_bytes=40 * 2**20
        ),
    )(cycle_cells, cycle_offsets, cycle_strength.reshape(1, CYC), block_tile.reshape(1, -1))
    displacement, diffused, renewed = pl.pallas_call(
        write_out,
        out_shape=shapes,
        in_specs=[vmem] * 3,
        out_specs=[hbm] * 3,
        scratch_shapes=[dma((4,))],
        compiler_params=pltpu.CompilerParams(vmem_limit_bytes=2**20),
    )(*results)
    return displacement, diffused, renewed.reshape(CYC)


def solution(mesh):
    in_specs = (
        P(None, ("row", "col")),
        P(None, ("row", "col")),
        P(("row", "col")),
        P(("row", "col")),
    )
    out_specs = (P(None, ("row", "col")), P("col", "row"), P(("row", "col")))
    return jax.shard_map(
        on_device, mesh=mesh, in_specs=in_specs, out_specs=out_specs, check_vma=False
    )
```
